256 devices in a mesh: dp: 64 (over z_hi, y, x, core), tensor: 4 (over z_lo).
Axes of the slice: x: 4, y: 4, z: 8 (z_hi: 2, z_lo: 4; z = z_hi * 4 + z_lo), core: 2. Of those that a mesh axis runs over, the one named last changes fastest.
Arguments:
- projection_input: bfloat16 [32768, 8192], P(('dp', 'tensor')), may hold values from -24 to 24
- rank_activations: bfloat16 [32768, 256], P('dp'), may hold values from -16 to 16
- projection_output_gradient: bfloat16 [32768, 8192], P('dp', 'tensor'), may hold values from -6 to 6
- down_factor: bfloat16 [8192, 256], replicated, may hold values from -0.375 to 0.375
- up_factor: bfloat16 [256, 8192], P(None, 'tensor'), may hold values from -0.0625 to 0.0625
- sparse_block_values: bfloat16 [4, 64, 64, 64], P('tensor'), may hold values from -0.75 to 0.75
- slot_block_rows: int32 [4, 64], P('tensor'), may hold values from 0 to 127, as said below
- slot_block_columns: int32 [4, 64], P('tensor'), may hold values from 0 to 31, as said below
- shard_block_count: int32 [4], P('tensor'), may hold values from 16 to 64, as said below
Outputs:
- grad_down: float32 [8192, 256], P('dp')
- up_factor_gradient: float32 [256, 8192], P('dp', 'tensor')
- grad_delta: float32 [4, 64, 64, 64], P('tensor')
- grad_input: bfloat16 [32768, 8192], P(('dp', 'tensor'))
The draws below stay inside these ranges and needn't reach their ends.
Inputs may be any that keep to these rules, and one draw needn't show every extreme that they name: `slot_block_rows`: within a shard no two slots name the same block (same row and column). `slot_block_columns`: columns count blocks inside the shard's own 8192 / 4 outputs. `shard_block_count`: some shard uses all 64 slots in every draw.
All inputs are finite; a program needn't handle non-finite values.
Results may differ from the reference program's by a relative error of at most 0.017.
Values may be sent and summed in bfloat16 or wider, within the bound.
No kernel may reach another device: no remote copies, remote signals or barrier semaphores. Data moves between devices by JAX's collectives and lax.ppermute only.
A program may use at most 128 MiB of HBM per device.

```python
import jax
import jax.numpy as jnp
from jax import lax

MODEL_WIDTH = 8192
QUERY_WIDTH = 8192
ADAPTER_RANK = 256
BLOCK = 64
SLOTS = 64
TOKEN_TOTAL = 32768
SHARDS = 4
RBLK = 128
CBLK = 32


def block_layout(key):
    shard_keys = jax.random.split(key, SHARDS)
    return jax.vmap(lambda one_key: jax.random.permutation(one_key, RBLK * CBLK)[:SLOTS])(shard_keys)


def draw_slot_block_rows(key, part):
    places = block_layout(key)
    return (places // CBLK).astype(jnp.int32)


def draw_slot_block_columns(key, part):
    places = block_layout(key)
    return (places % CBLK).astype(jnp.int32)


def draw_shard_block_count(key, part):
    key = jax.random.fold_in(key, 7)
    first_key, second_key = jax.random.split(key)
    counts = jax.random.randint(first_key, (SHARDS,), SLOTS // 4, SLOTS + 1)
    fullest = jax.random.randint(second_key, (), 0, SHARDS)
    return jnp.where(jnp.arange(SHARDS) == fullest, SLOTS, counts).astype(jnp.int32)


def spiked(entries, key, source, target, parts, factor):
    owner, partner = [(jnp.arange(entries.shape[axis_at]) // (entries.shape[axis_at] // parts)).reshape([-1 if axis == axis_at else 1 for axis in range(entries.ndim)]) for axis_at in (source, target)]
    chosen = jax.random.permutation(key, parts)[partner]
    strong = (owner == chosen) | (owner == (partner + parts // 2) % parts)
    return jnp.where(strong, factor * entries, entries)


def block_levels(key, shape, cuts, least, largest):
    level, own = 1.0, jax.random.fold_in(key, 6)
    for position, shards_of in cuts:
        draws = jnp.exp(jax.random.uniform(jax.random.fold_in(own, position), (shards_of,), jnp.float32, least / len(cuts), largest / len(cuts)))
        level = level * jnp.repeat(draws, shape[position] // shards_of).reshape([-1 if axis == position else 1 for axis in range(len(shape))])
    return level


def centred(key, extent, scale, most, cuts=(), kind=jnp.bfloat16):
    array = jax.random.normal(key, extent, jnp.float32) * scale
    if len(cuts) > 0:
        array = block_levels(key, extent, cuts, -0.22, 0.18) * array
    return jnp.clip(array, min=-most, max=most).astype(kind)


def gaussian_with(own_key, shape, scale, reach, cuts, heavy, dtype=jnp.bfloat16):
    array = scale * jax.random.normal(own_key, shape, jnp.float32)
    if cuts:
        array = array * block_levels(own_key, shape, cuts, -0.22, 0.18)
    return jnp.clip(spiked(array, jax.random.fold_in(own_key, 3), *heavy), -reach, reach).astype(dtype)


def setup_inputs(seed: int = 0) -> dict:
    keys = jax.random.split(jax.random.key(seed), 10)
    return {
        "projection_input": gaussian_with(keys[0], (TOKEN_TOTAL, MODEL_WIDTH), 1.0, 24.0, ((0, 256),), (0, 1, 256, 6.0)),
        "rank_activations": gaussian_with(keys[1], (TOKEN_TOTAL, ADAPTER_RANK), 1.0, 16.0, ((0, 64),), (0, 1, 64, 4.0)),
        "projection_output_gradient": centred(keys[2], (TOKEN_TOTAL, QUERY_WIDTH), 1.0, 6.0, ((0, 64), (1, 4))),
        "down_factor": centred(keys[3], (MODEL_WIDTH, ADAPTER_RANK), ADAPTER_RANK ** -0.5, 0.375),
        "up_factor": centred(keys[4], (ADAPTER_RANK, QUERY_WIDTH), QUERY_WIDTH ** -0.5, 0.0625, ((1, 4),)),
        "sparse_block_values": centred(keys[5], (SHARDS, SLOTS, BLOCK, BLOCK), BLOCK ** -0.5, 0.75, ((0, 4),)),
        "slot_block_rows": draw_slot_block_rows(jax.random.fold_in(keys[9], 71), 0),
        "slot_block_columns": draw_slot_block_columns(jax.random.fold_in(keys[9], 71), 0),
        "shard_block_count": draw_shard_block_count(jax.random.fold_in(keys[9], 71), 0),
    }


def reference(projection_input, rank_activations, projection_output_gradient, down_factor, up_factor, sparse_block_values, slot_block_rows, slot_block_columns, shard_block_count):
    shard_width = QUERY_WIDTH // SHARDS
    rank_gradient = lax.dot_general(projection_output_gradient, up_factor, (((1,), (1,)), ((), ())), preferred_element_type=jnp.float32).astype(jnp.bfloat16)
    grad_down = lax.dot_general(projection_input, rank_gradient, (((0,), (0,)), ((), ())), preferred_element_type=jnp.float32)
    up_factor_gradient = lax.dot_general(rank_activations, projection_output_gradient, (((0,), (0,)), ((), ())), preferred_element_type=jnp.float32)
    blocked_input = projection_input.reshape(TOKEN_TOTAL, RBLK, BLOCK)
    slot_ids = jnp.arange(SLOTS)
    grand_total = lax.dot_general(rank_gradient, down_factor, (((1,), (1,)), ((), ())), preferred_element_type=jnp.float32)
    grads_list = []
    for shard in range(SHARDS):
        rows_here = slot_block_rows[shard]
        cols_here = slot_block_columns[shard]
        live_mask = (slot_ids < shard_block_count[shard]).astype(jnp.float32)
        input_pick = blocked_input[:, rows_here, :].astype(jnp.float32)
        shard_grad = projection_output_gradient[:, shard * shard_width:(shard + 1) * shard_width].reshape(TOKEN_TOTAL, CBLK, BLOCK)
        grad_pick = shard_grad[:, cols_here, :].astype(jnp.float32)
        block_grad = jnp.einsum("nsk,nsj->skj", input_pick, grad_pick, precision=lax.Precision.HIGHEST)
        grads_list.append(block_grad * live_mask[:, None, None])
        spread = jnp.einsum("nsj,skj->nsk", grad_pick, sparse_block_values[shard].astype(jnp.float32), precision=lax.Precision.HIGHEST)
        spread = spread * live_mask[None, :, None]
        shard_part = jnp.zeros((TOKEN_TOTAL, RBLK, BLOCK), jnp.float32).at[:, rows_here, :].add(spread)
        shard_part = lax.optimization_barrier(shard_part.astype(jnp.bfloat16))
        grand_total = grand_total + shard_part.reshape(TOKEN_TOTAL, MODEL_WIDTH).astype(jnp.float32)
    grad_delta = jnp.stack(grads_list, axis=0)
    grad_input = grand_total.astype(jnp.bfloat16)
    return grad_down, up_factor_gradient, grad_delta, grad_input
```

```python
import functools

import jax
import jax.numpy as jnp
from jax import lax
from jax.experimental import pallas as pl
from jax.experimental.pallas import tpu as pltpu
from jax.sharding import Mesh, PartitionSpec as P

F32 = jnp.float32
BF16 = jnp.bfloat16
ZH, Y, X, C, T = 2, 4, 4, 2, 4
XY = Y * X
DP = ("zh", "y", "x", "c")
ALL = DP + ("t",)
BLK = 64
TOK = 128
PAIRS = 32
VMEM_LIMIT = 48 * 1024 * 1024


def block_rows(ref, index):
    return ref[pl.ds(pl.multiple_of(index * BLK, BLK), BLK), :]


def delta_kernel(rows, cols, cnt, x_ref, g_ref, out_ref, gt_ref, xt_ref):
    def turn(i, carry):
        at = pl.multiple_of(i * 128, 128)
        xt_ref[pl.ds(at, 128), :] = x_ref[:, pl.ds(at, 128)].T
        return carry

    lax.fori_loop(0, x_ref.shape[1] // 128, turn, 0, unroll=4)
    width = g_ref.shape[2]
    for t in range(T):

        def turn_g(i, carry):
            at = pl.multiple_of(i * 128, 128)
            gt_ref[pl.ds(t * width + at, 128), :] = g_ref[t, :, pl.ds(at, 128)].T
            return carry

        lax.fori_loop(0, width // 128, turn_g, 0, unroll=4)

    lane = lax.broadcasted_iota(jnp.int32, (BLK, 2 * BLK), 1)
    per_shard = width // BLK

    def pair(p, carry):
        for t in range(T):
            s0, s1 = p, p + PAIRS
            xt = jnp.concatenate(
                [block_rows(xt_ref, rows[t, s0]), block_rows(xt_ref, rows[t, s1])], axis=0
            )
            gt = jnp.concatenate(
                [
                    block_rows(gt_ref, cols[t, s0] + t * per_shard),
                    block_rows(gt_ref, cols[t, s1] + t * per_shard),
                ],
                axis=0,
            )
            full = lax.dot_general(xt, gt, (((1,), (1,)), ((), ())), preferred_element_type=F32)
            live = jnp.where(lane < BLK, s0, s1) < cnt[t, 0]
            both = jnp.where(lane < BLK, full[:BLK], full[BLK:])
            out_ref[p, t] = jnp.where(live, both, 0.0).astype(BF16)
        return carry

    lax.fori_loop(0, PAIRS, pair, 0, unroll=2)


def input_kernel(rows, cols, cnt, low_ref, down_ref, gt_ref, v_ref, out_ref, acc_ref):
    low = low_ref[...]
    step = 512

    def dense(i, carry):
        at = pl.multiple_of(i * step, step)
        acc_ref[pl.ds(at, step), :] = lax.dot_general(
            down_ref[pl.ds(at, step), :], low, (((1,), (1,)), ((), ())), preferred_element_type=F32
        )
        return carry

    lax.fori_loop(0, acc_ref.shape[0] // step, dense, 0, unroll=2)
    lane = lax.broadcasted_iota(jnp.int32, (BLK, 2 * BLK), 1)
    per_shard = gt_ref.shape[0] // T // BLK

    def pair(p, carry):
        s0, s1 = p, p + PAIRS
        parts = []
        for t in range(T):
            v = v_ref[t, p]
            zero = jnp.zeros_like(v)
            top = jnp.where((lane < BLK) & (s0 < cnt[t, 0]), v, zero)
            bottom = jnp.where((lane >= BLK) & (s1 < cnt[t, 0]), v, zero)
            gt = jnp.concatenate(
                [
                    block_rows(gt_ref, cols[t, s0] + t * per_shard),
                    block_rows(gt_ref, cols[t, s1] + t * per_shard),
                ],
                axis=0,
            )
            parts.append(
                jnp.dot(
                    jnp.concatenate([top, bottom], axis=0), gt, preferred_element_type=F32
                )
            )
        for t in range(T):
            for s, part in ((s0, parts[t][:BLK]), (s1, parts[t][BLK:])):
                at = pl.ds(pl.multiple_of(rows[t, s] * BLK, BLK), BLK)
                acc_ref[at, :] = acc_ref[at, :] + part
        return carry

    lax.fori_loop(0, PAIRS, pair, 0, unroll=2)

    def turn(i, carry):
        at = pl.multiple_of(i * 128, 128)
        out_ref[:, pl.ds(at, 128)] = acc_ref[pl.ds(at, 128), :].T.astype(BF16)
        return carry

    lax.fori_loop(0, acc_ref.shape[0] // 128, turn, 0, unroll=4)


def whole():
    return pl.BlockSpec(memory_space=pltpu.VMEM)


def scalars():
    return pl.BlockSpec(memory_space=pltpu.SMEM)


def ring(shift_of_core):
    def place(z, c):
        return (z // T * C + c) * T + z % T

    n = ZH * T
    return [
        (place(z, c), place((z + shift_of_core[c]) % n, c)) for z in range(n) for c in range(C)
    ]


def swap(array):
    return lax.ppermute(array, "c", [(0, 1), (1, 0)])


def per_device(x_own, acts, grad, down, up, values, slot_rows, slot_cols, count):
    c = lax.axis_index("c")
    t = lax.axis_index("t")
    feat = x_own.shape[1]
    width = grad.shape[1]
    rank = up.shape[0]

    grad_own = lax.all_to_all(grad.reshape(T, TOK, width), "t", 0, 0, tiled=True)

    table = jnp.concatenate(
        [slot_rows, slot_cols, jnp.broadcast_to(count[:, None], (1, 128))], axis=1
    )
    tables = lax.all_gather(table, "t", axis=0, tiled=True)
    rows4, cols4, cnt4 = tables[:, :64], tables[:, 64:128], tables[:, 128:]

    packed = jnp.concatenate([values[0, :PAIRS], values[0, PAIRS:]], axis=2)
    half = lax.dynamic_slice_in_dim(packed, c * (PAIRS // C), PAIRS // C, 0)
    axes = ("zh", "c", "t")
    from_prev = lax.ppermute(half, axes, ring((1, 1)))
    from_next = lax.ppermute(half, axes, ring((-1, -1)))
    from_far = lax.ppermute(half, axes, ring((2, -2)))
    got = jnp.stack([from_prev, from_far, from_next])
    got_too = swap(got)
    others = jnp.where(c == 0, jnp.concatenate([got, got_too], 1), jnp.concatenate([got_too, got], 1))
    ordered = jnp.concatenate([packed[None], others], 0)
    values4 = jnp.take(ordered, (t - jnp.arange(T)) % T, axis=0)

    x_view = x_own.reshape(TOK, ZH, Y, X, C, 128)
    x_keep = lax.dynamic_index_in_dim(x_view, c, 4, keepdims=False)
    x_give = lax.dynamic_index_in_dim(x_view, 1 - c, 4, keepdims=False)
    x_got = swap(x_give)

    low_part = lax.dot_general(grad, up, (((1,), (1,)), ((), ())), preferred_element_type=F32)
    low_parts = lax.all_to_all(
        low_part.astype(BF16).reshape(T, TOK, rank), "t", 0, 0, tiled=True
    )
    low = jnp.sum(low_parts.astype(F32), axis=0).astype(BF16)
    low_got = swap(low)

    acts_view = acts.reshape(acts.shape[0], ZH, XY, C, 4).transpose(0, 3, 2, 1, 4)
    up_part = lax.dot_general(
        acts_view.reshape(acts.shape[0], rank), grad, (((0,), (0,)), ((), ())),
        preferred_element_type=F32,
    ).astype(BF16).reshape(C, XY, ZH * 4, width)
    up_keep = lax.dynamic_index_in_dim(up_part, c, 0, keepdims=False)
    up_got = swap(lax.dynamic_index_in_dim(up_part, 1 - c, 0, keepdims=False))
    up_half = (up_keep.astype(F32) + up_got.astype(F32)).astype(BF16)
    up_sum = jnp.sum(
        lax.all_to_all(up_half, ("y", "x"), 0, 0, tiled=True).astype(F32), axis=0
    ).reshape(ZH, 4, width)
    zh = lax.axis_index("zh")
    up_far = lax.ppermute(
        lax.dynamic_index_in_dim(up_sum, 1 - zh, 0, keepdims=False), "zh", [(0, 1), (1, 0)]
    )
    up_grad = lax.dynamic_index_in_dim(up_sum, zh, 0, keepdims=False) + up_far

    form = "nzyxk,nr->yxzkr"
    down_part = jnp.einsum(form, x_keep, low, preferred_element_type=F32) + jnp.einsum(
        form, x_got, low_got, preferred_element_type=F32
    )
    down_part = down_part.astype(BF16).reshape(XY, ZH * 128, rank)
    down_sum = jnp.sum(
        lax.all_to_all(down_part, ("y", "x"), 0, 0, tiled=True).astype(F32), axis=0
    ).astype(BF16).reshape(ZH, 1, 128, rank)
    down_all = lax.all_to_all(
        jnp.broadcast_to(down_sum, (ZH, T, 128, rank)).reshape(ZH * T, 128, rank),
        ("zh", "t"), 0, 0, tiled=True,
    )
    down_grad = jnp.sum(down_all.astype(F32), axis=0)

    params = pltpu.CompilerParams(vmem_limit_bytes=VMEM_LIMIT)
    delta_part, grad_t = pl.pallas_call(
        delta_kernel,
        out_shape=(
            jax.ShapeDtypeStruct((PAIRS, T, BLK, 2 * BLK), BF16),
            jax.ShapeDtypeStruct((T * width, TOK), BF16),
        ),
        in_specs=[scalars()] * 3 + [whole()] * 2,
        out_specs=(whole(), whole()),
        scratch_shapes=[pltpu.VMEM((feat, TOK), BF16)],
        compiler_params=params,
        cost_estimate=pl.CostEstimate(flops=4 << 30, bytes_accessed=8 << 20, transcendentals=0),
        name="delta",
    )(rows4, cols4, cnt4, x_own, grad_own)
    delta_view = delta_part.reshape(XY, C, T * BLK, 2 * BLK)
    delta_keep = lax.dynamic_index_in_dim(delta_view, c, 1, keepdims=False)
    delta_got = swap(lax.dynamic_index_in_dim(delta_view, 1 - c, 1, keepdims=False))
    delta_half = (delta_keep.astype(F32) + delta_got.astype(F32)).astype(BF16)
    delta_sum = jnp.sum(
        lax.all_to_all(delta_half, ("y", "x"), 0, 0, tiled=True).astype(F32), axis=0
    ).astype(BF16).reshape(1, T, BLK, 2 * BLK)
    delta_all = lax.all_to_all(
        jnp.broadcast_to(delta_sum, (ZH, T, BLK, 2 * BLK)).reshape(ZH * T, BLK, 2 * BLK),
        ("zh", "t"), 0, 0, tiled=True,
    )
    delta_one = jnp.sum(delta_all.astype(F32), axis=0, keepdims=True).astype(BF16)
    delta_full = lax.all_gather(delta_one, ("y", "x", "c"), axis=0, tiled=True).astype(F32)
    grad_delta = jnp.concatenate([delta_full[:, :, :BLK], delta_full[:, :, BLK:]], 0)[None]

    grad_input = pl.pallas_call(
        input_kernel,
        out_shape=jax.ShapeDtypeStruct((TOK, feat), BF16),
        in_specs=[scalars()] * 3 + [whole()] * 4,
        out_specs=whole(),
        scratch_shapes=[pltpu.VMEM((feat, TOK), F32)],
        compiler_params=params,
        cost_estimate=pl.CostEstimate(flops=5 << 30, bytes_accessed=12 << 20, transcendentals=0),
        name="grad_input",
    )(rows4, cols4, cnt4, low, down, grad_t, values4)
    return down_grad, up_grad, grad_delta, grad_input


def solution(mesh):
    fine = Mesh(mesh.devices.reshape(ZH, Y, X, C, T), ALL)
    return jax.shard_map(
        per_device,
        mesh=fine,
        in_specs=(
            P(ALL, None),
            P(DP, None),
            P(DP, "t"),
            P(),
            P(None, "t"),
            P("t", None, None, None),
            P("t", None),
            P("t", None),
            P("t"),
        ),
        out_specs=(
            P(DP, None),
            P(DP, "t"),
            P("t", None, None, None),
            P(ALL, None),
        ),
        check_vma=False,
    )
```

```python
import functools

import jax
import jax.numpy as jnp
from jax import lax
from jax.experimental import pallas as pl
from jax.experimental.pallas import tpu as pltpu
from jax.sharding import Mesh, PartitionSpec as P

F32 = jnp.float32
BF16 = jnp.bfloat16
ZH, Y, X, C, T = 2, 4, 4, 2, 4
XY = Y * X
DP = ("zh", "y", "x", "c")
ALL = DP + ("t",)
BLK = 64
TOK = 128
SLOTS = 64
PAIRS = SLOTS // 2
LANES_OVER = (((1,), (1,)), ((), ()))
MIB = 1024 * 1024


GUESS = {"delta_last": 8.0, "delta_most": 0.0, "low": 10.0, "grad_input": 0.0, "stage": 0.0, "pack": 0.0, "values": 0.0}


def whole():
    return pl.BlockSpec(memory_space=pltpu.VMEM)


def scalars():
    return pl.BlockSpec(memory_space=pltpu.SMEM)


def anywhere():
    return pl.BlockSpec(memory_space=pl.ANY)


def aligned(index, size):
    return pl.ds(pl.multiple_of(index * size, size), size)


def turn_kernel(x_hbm, after_ref, out_ref, x_ref, sems):
    step = x_ref.shape[1] // 8
    copies = []
    for i in range(8):
        at = pl.ds(i * step, step)
        copies.append(pltpu.make_async_copy(x_hbm.at[:, at], x_ref.at[:, at], sems.at[i]))
    for copy in copies:
        copy.start()
    for i in range(8):
        copies[i].wait()
        for j in range(i * step, i * step + step, 128):
            out_ref[j : j + 128, :] = x_ref[:, j : j + 128].T


def front_kernel(place, count, *refs):
    from_hbm, lows, pieces = refs[:4], refs[4 : 4 + T], refs[4 + T : 4 + 2 * T]
    grad_ref, up_ref, rows_ref, cols_ref, low_ref, sems = refs[4 + 2 * T :]
    copies = [
        pltpu.make_async_copy(there, here, sems.at[i])
        for i, (there, here) in enumerate(zip(from_hbm, (grad_ref, up_ref, rows_ref, cols_ref)))
    ]
    for copy in copies:
        copy.start()
    copies[0].wait()
    gives = []
    for k in range(T):
        at = pl.ds(pl.multiple_of((place[4] ^ k) * TOK, TOK), TOK)
        gives.append(pltpu.make_async_copy(grad_ref.at[at], pieces[k], sems.at[4 + k]))
    for give in gives:
        give.start()
    for copy in copies[1:]:
        copy.wait()
    low_ref[...] = lax.dot_general(
        grad_ref[...], up_ref[...], LANES_OVER, preferred_element_type=F32
    ).astype(BF16)
    line = jnp.concatenate(
        [rows_ref[...], cols_ref[...], jnp.full((1, 2 * SLOTS), count[0], jnp.int32)], axis=1
    ).astype(F32)
    line = jnp.broadcast_to(line, (16, line.shape[1])).astype(BF16)
    for k in range(T):
        lows[k][:TOK] = low_ref[aligned(place[4] ^ k, TOK), :]
        lows[k][TOK:] = line
    for give in gives:
        give.wait()


def up_kernel(grad_hbm, acts_hbm, out_ref, grad_ref, acts_ref, sems):
    copies = [
        pltpu.make_async_copy(acts_hbm, acts_ref, sems.at[0]),
        pltpu.make_async_copy(grad_hbm, grad_ref, sems.at[1]),
    ]
    for copy in copies:
        copy.start()
    copies[0].wait()
    rank = acts_ref.shape[1]
    here = lax.broadcasted_iota(jnp.int32, (rank, rank), 1)
    chunk, zh = here >> 3, (here >> 2) & 1
    order = lax.broadcasted_iota(jnp.int32, (rank, rank), 0) == (
        ((zh * (XY * C) + chunk) << 2) + (here & 3)
    )
    order = jnp.where(order, 1.0, 0.0).astype(BF16)
    acts = jnp.dot(acts_ref[...], order, preferred_element_type=F32).astype(BF16)
    copies[1].wait()
    step = 512

    def columns(i, carry):
        out_ref[:, aligned(i, step)] = lax.dot_general(
            acts, grad_ref[:, aligned(i, step)], (((0,), (0,)), ((), ())),
            preferred_element_type=F32,
        ).astype(BF16)
        return carry

    lax.fori_loop(0, grad_ref.shape[1] // step, columns, 0, unroll=2)


def low_kernel(*refs):
    low_ref, table_ref = refs[-2:]
    total = refs[0][:TOK].astype(F32)
    for piece in refs[1:T]:
        total += piece[:TOK].astype(F32)
    low_ref[...] = total.astype(BF16)
    for k in range(T):
        table_ref[k * 8 : k * 8 + 8] = refs[k][TOK:].astype(F32).astype(jnp.int32)[:8]


def pass_kernel(*refs):
    pass


def pack_kernel(values_ref, after_ref, out_ref):
    def one(p, carry):
        out_ref[p] = jnp.concatenate([values_ref[p], values_ref[p + PAIRS]], axis=1)
        return carry

    lax.fori_loop(0, PAIRS, one, 0, unroll=4)


def down_sum_kernel(place, down_ref, keep_ref, give_ref):
    rows = down_ref.shape[1] // ZH
    for mine in range(2):
        zh = place[5] ^ (1 - mine)
        at = aligned(zh, rows)
        total = down_ref[0, at, :].astype(F32)
        for i in range(1, XY):
            total += down_ref[i, at, :].astype(F32)
        if mine:
            keep_ref[...] = total
        else:
            give_ref[...] = total.astype(BF16)


def down_half_kernel(keep_ref, far_ref, out_ref):
    out_ref[...] = (keep_ref[...] + far_ref[...].astype(F32)).astype(BF16)


def down_last_kernel(*refs):
    total = refs[0][...].astype(F32)
    for part in refs[1:T]:
        total += part[...].astype(F32)
    refs[-1][...] = total


def stage_kernel(place, delta_ref, after_ref, out_ref, sum_ref):
    for k in range(T):
        total = delta_ref[0, k].astype(F32)
        for i in range(1, XY):
            total += delta_ref[i, k].astype(F32)
        sum_ref[k] = total
    for t in range(T):
        part = sum_ref[place[4] ^ t].astype(BF16)
        for zh in range(ZH):
            out_ref[zh * T + t] = part


def last_kernel(parts_ref, after_ref, after_too_ref, delta_ref):
    total = parts_ref[0].astype(F32)
    for i in range(1, ZH * T):
        total += parts_ref[i].astype(F32)
    delta = total.astype(BF16)
    for p in range(PAIRS):
        delta_ref[p] = delta


def unpack_kernel(pairs_ref, out_ref):
    def one(p, carry):
        pair = pairs_ref[p].astype(F32)
        out_ref[p] = pair[:, :BLK]
        out_ref[p + PAIRS] = pair[:, BLK:]
        return carry

    lax.fori_loop(0, PAIRS, one, 0, unroll=4)


def down_kernel(place, xt_ref, xt_far_ref, low_ref, low_far_ref, *refs):
    out_ref = refs[-1]
    low, low_far = low_ref[...], low_far_ref[...]
    core = place[0]

    def block(i, carry):
        for zh in range(ZH):
            at = aligned((zh * XY + i) * C + core, 128)
            total = jnp.dot(xt_ref[at, :], low, preferred_element_type=F32)
            total += jnp.dot(xt_far_ref[at, :], low_far, preferred_element_type=F32)
            out_ref[i, zh * 128 : (zh + 1) * 128] = total.astype(BF16)
        return carry

    lax.fori_loop(0, XY, block, 0, unroll=4)


def delta_kernel(pieces, place, table, xt_ref, xt_far_ref, *refs):
    n = len(pieces)
    near, far = refs[:n], refs[n : 2 * n]
    all_ref, grad_ref, out_ref, gt_ref, both_ref, sems = refs[-6:]
    width = near[0].shape[1]
    core = place[0]
    for j in range(n):

        def turn(i, carry, j=j):
            at = pl.ds(pl.multiple_of(i * 128, 128), 128)
            own = near[j][:, at].T
            both_ref[at, j * 256 : j * 256 + 128] = own
            both_ref[at, j * 256 + 128 : j * 256 + 256] = far[j][:, at].T
            gt_ref[pl.ds(pl.multiple_of(j * width + i * 128, 128), 128), :] = own
            return carry

        lax.fori_loop(0, width // 128, turn, 0, unroll=4)
    keep = pltpu.make_async_copy(gt_ref, grad_ref, sems.at[0])
    keep.start()

    lane = lax.broadcasted_iota(jnp.int32, (BLK, 2 * BLK), 1)

    def rows_of(index):
        return jnp.concatenate(
            [xt_ref[aligned(index, BLK), :], xt_far_ref[aligned(index, BLK), :]], axis=1
        )

    def pair(i, carry):
        s0 = i * C + core
        s1 = s0 + PAIRS
        for j, k in enumerate(pieces):
            xt = jnp.concatenate([rows_of(table[8 * k, s0]), rows_of(table[8 * k, s1])], axis=0)
            gt = jnp.concatenate(
                [
                    both_ref[aligned(table[8 * k, SLOTS + s], BLK), j * 256 : j * 256 + 256]
                    for s in (s0, s1)
                ],
                axis=0,
            )
            full = lax.dot_general(xt, gt, LANES_OVER, preferred_element_type=F32)
            live = jnp.where(lane < BLK, s0, s1) < table[8 * k, 2 * SLOTS]
            both = jnp.where(lane < BLK, full[:BLK], full[BLK:])
            out_ref[i, j] = jnp.where(live, both, 0.0).astype(BF16)
        return carry

    lax.fori_loop(0, XY, pair, 0, unroll=4)
    give = pltpu.make_async_copy(out_ref, all_ref.at[:, pieces[0] : pieces[0] + n], sems.at[1])
    give.start()
    keep.wait()
    give.wait()


def input_kernel(place, table, low_ref, *refs):
    from_hbm = refs[:7]
    out_ref, acc_ref, down_ref, gt_ref, values, sems = refs[7:]
    most = from_hbm[1].shape[0]
    to_vmem = (
        down_ref, gt_ref.at[:most], gt_ref.at[most:], values.at[0], values.at[1], values.at[2], values.at[3],
    )
    copies = [
        pltpu.make_async_copy(there, here, sems.at[n])
        for n, (there, here) in enumerate(zip(from_hbm, to_vmem))
    ]
    for copy in copies:
        copy.start()
    low = low_ref[...]
    step = 512
    width = gt_ref.shape[0] // T

    def dense(i, carry):
        acc_ref[aligned(i, step), :] = lax.dot_general(
            down_ref[aligned(i, step), :], low, LANES_OVER, preferred_element_type=F32
        )
        return carry

    copies[0].wait()
    lax.fori_loop(0, acc_ref.shape[0] // step, dense, 0, unroll=2)
    for copy in copies[1:]:
        copy.wait()
    lane = lax.broadcasted_iota(jnp.int32, (BLK, 2 * BLK), 1)

    def product(v, k, s0, s1):
        zero = jnp.zeros_like(v)
        live = table[8 * k, 2 * SLOTS]
        top = jnp.where((lane < BLK) & (s0 < live), v, zero)
        bottom = jnp.where((lane >= BLK) & (s1 < live), v, zero)
        gt = jnp.concatenate(
            [
                gt_ref[aligned(table[8 * k, SLOTS + s] + k * (width // BLK), BLK), :]
                for s in (s0, s1)
            ],
            axis=0,
        )
        return jnp.dot(jnp.concatenate([top, bottom], axis=0), gt, preferred_element_type=F32)

    def pair(i, carry):
        done = []
        for s0 in (2 * i, 2 * i + 1):
            s1 = s0 + PAIRS
            for m in range(T):
                k = 0 if m == 0 else place[m]
                done.append((k, s0, s1, product(values[m, s0], k, s0, s1)))
        for k, s0, s1, part in done:
            for s, add in ((s0, part[:BLK]), (s1, part[BLK:])):
                at = aligned(table[8 * k, s], BLK)
                acc_ref[at, :] = acc_ref[at, :] + add
        return carry

    lax.fori_loop(0, PAIRS // 2, pair, 0)

    def turn(i, carry):
        out_ref[:, aligned(i, 128)] = acc_ref[aligned(i, 128), :].T.astype(BF16)
        return carry

    lax.fori_loop(0, acc_ref.shape[0] // 128, turn, 0, unroll=4)


def ring(shift_of_core):
    def place(z, c):
        return (z // T * C + c) * T + z % T

    n = ZH * T
    return [
        (place(z, c), place((z + shift_of_core[c]) % n, c)) for z in range(n) for c in range(C)
    ]


def swap(array, axis="c"):
    return lax.ppermute(array, axis, [(0, 1), (1, 0)])


def cross(array, k):
    return lax.ppermute(array, "t", [(i, i ^ k) for i in range(T)])


def call(kernel, name, outs, in_specs, *args, out_specs=None, scratch=(), room=16, **grid):
    return pl.pallas_call(
        kernel,
        out_shape=outs,
        in_specs=in_specs,
        out_specs=out_specs if out_specs is not None else jax.tree.map(lambda _: whole(), outs),
        scratch_shapes=scratch,
        compiler_params=pltpu.CompilerParams(vmem_limit_bytes=room * MIB),
        cost_estimate=pl.CostEstimate(
            flops=int(GUESS.get(name, 0) * 1000000000) + 1024, bytes_accessed=1024, transcendentals=0
        ),
        name=name,
        **grid,
    )(*args)


def per_device(x_own, acts, grad, down, up, values, slot_rows, slot_cols, count):
    zh, c, t = lax.axis_index("zh"), lax.axis_index("c"), lax.axis_index("t")
    feat, width, rank = x_own.shape[1], grad.shape[1], up.shape[0]
    place = jnp.stack(
        [c, t ^ ((t - 1) % T), t ^ ((t + 1) % T), 2 + 0 * t, t, zh]
    ).astype(jnp.int32)
    rows = TOK + 16
    shape = jax.ShapeDtypeStruct

    given = call(
        front_kernel, "front",
        (shape((rows, rank), BF16),) * T + (shape((TOK, width), BF16),) * T,
        [scalars()] * 2 + [anywhere()] * 4, place, count, grad, up, slot_rows, slot_cols,
        out_specs=(whole(),) * T + (anywhere(),) * T, room=56,
        scratch=[
            pltpu.VMEM(grad.shape, BF16),
            pltpu.VMEM(up.shape, BF16),
            pltpu.VMEM((1, SLOTS), jnp.int32),
            pltpu.VMEM((1, SLOTS), jnp.int32),
            pltpu.VMEM((T * TOK, rank), BF16),
            pltpu.SemaphoreType.DMA((4 + T,)),
        ],
    )
    parts, near = given[:T], given[T:]
    parts = [parts[0]] + [cross(parts[k], k) for k in (1, 2, 3)]
    near = [near[0]] + [cross(near[k], k) for k in (1, 2, 3)]

    xt = call(
        turn_kernel, "turn_input", shape((feat, TOK), BF16),
        [anywhere()] * 2, x_own, given[0],
        scratch=[pltpu.VMEM(x_own.shape, BF16), pltpu.SemaphoreType.DMA((8,))],
    )
    xt_far = swap(xt)

    up_part = call(
        up_kernel, "up_part", shape((rank, width), BF16), [anywhere()] * 2, grad, acts,
        scratch=[
            pltpu.VMEM(grad.shape, BF16),
            pltpu.VMEM(acts.shape, BF16),
            pltpu.SemaphoreType.DMA((2,)),
        ],
    )

    low, table = call(
        low_kernel, "low", (shape((TOK, rank), BF16), shape((8 * T, rank), jnp.int32)),
        [whole()] * T + [anywhere()], *parts, up_part,
    )
    low_far = swap(low)

    up_all = lax.all_to_all(
        up_part.reshape(XY * C, ZH * 4, width), ("y", "x", "c"), 0, 0, tiled=True
    )
    up_sum = jnp.sum(up_all.astype(F32), axis=0).reshape(ZH, 4, width)
    up_far = swap(lax.dynamic_index_in_dim(up_sum, 1 - zh, 0, keepdims=False), "zh")
    up_grad = lax.dynamic_index_in_dim(up_sum, zh, 0, keepdims=False) + up_far

    down_part = call(
        down_kernel, "down_part", shape((XY, ZH * 128, rank), BF16),
        [scalars()] + [whole()] * 4 + [anywhere()], place, xt, xt_far, low, low_far,
        up_all,
    )
    down_all = lax.all_to_all(down_part, ("y", "x"), 0, 0, tiled=True)
    down_keep, down_give = call(
        down_sum_kernel, "down_sum", (shape((128, rank), F32), shape((128, rank), BF16)),
        [scalars(), whole()], place, down_all,
    )
    down_half = call(
        down_half_kernel, "down_half", shape((128, rank), BF16), [whole()] * 2,
        down_keep, swap(down_give, "zh"),
    )
    down_grad = call(
        down_last_kernel, "down_last", shape((128, rank), F32), [whole()] * T,
        down_half, *[cross(down_half, k) for k in (1, 2, 3)],
    )

    def delta_call(pieces, *before):
        n = len(pieces)
        return call(
            functools.partial(delta_kernel, pieces), "delta_last" if before else "delta_most",
            (shape((XY, T, BLK, 2 * BLK), BF16), shape((n * width, TOK), BF16)),
            [scalars()] * 2 + [whole()] * (2 + 2 * n) + [anywhere()] * len(before),
            place, table, xt, xt_far, *[near[k] for k in pieces], *[far[k] for k in pieces],
            *before,
            out_specs=(anywhere(), anywhere()), room=24,
            scratch=[
                pltpu.VMEM((XY, n, BLK, 2 * BLK), BF16),
                pltpu.VMEM((n * width, TOK), BF16),
                pltpu.VMEM((width, 256 * n), BF16),
                pltpu.SemaphoreType.DMA((2,)),
            ],
            input_output_aliases={4 + 2 * n: 0} if before else {},
        )

    far = [swap(near[k]) for k in (0, 1, 2)]
    delta_most, grad_most = delta_call((0, 1, 2))
    near[3] = call(
        pass_kernel, "gate", shape((TOK, width), BF16), [anywhere()] * 2, near[3], delta_most,
        out_specs=anywhere(), input_output_aliases={0: 0},
    )
    far.append(swap(near[3]))
    delta_full, grad_last = delta_call((3,), delta_most)
    delta_part = call(
        pass_kernel, "join", shape((XY, T, BLK, 2 * BLK), BF16), [anywhere()] * 2,
        delta_full, down_all,
        out_specs=anywhere(), input_output_aliases={0: 0},
    )
    delta_all = lax.all_to_all(delta_part, ("y", "x"), 0, 0, tiled=True)

    packed = call(
        pack_kernel, "pack", shape((PAIRS, BLK, 2 * BLK), BF16), [whole(), anywhere()],
        values[0], near[3],
    )
    axes = ("zh", "t")
    got = [
        lax.ppermute(packed, axes, [(i, (i + 1) % (ZH * T)) for i in range(ZH * T)]),
        lax.ppermute(packed, axes, [(i, (i - 1) % (ZH * T)) for i in range(ZH * T)]),
        lax.ppermute(packed, ("zh", "c", "t"), ring((2, -2))),
    ]
    got = call(
        pass_kernel, "values", (shape(packed.shape, BF16),) * 3, [anywhere()] * 3, *got,
        out_specs=(anywhere(),) * 3, input_output_aliases={0: 0, 1: 1, 2: 2},
    )
    grad_input = call(
        input_kernel, "grad_input", shape((TOK, feat), BF16),
        [scalars()] * 2 + [whole()] + [anywhere()] * 7,
        place, table, low, down, grad_most, grad_last, packed, *got, room=56,
        scratch=[
            pltpu.VMEM((feat, TOK), F32),
            pltpu.VMEM(down.shape, BF16),
            pltpu.VMEM((T * width, TOK), BF16),
            pltpu.VMEM((T, PAIRS, BLK, 2 * BLK), BF16),
            pltpu.SemaphoreType.DMA((7,)),
        ],
    )

    stage = call(
        stage_kernel, "stage", shape((ZH * T, BLK, 128), BF16),
        [scalars(), whole(), anywhere()], place, delta_all, down_give,
        scratch=[pltpu.VMEM((T, BLK, 2 * BLK), F32)],
    )
    stage_all = lax.all_to_all(stage, ("zh", "t"), 0, 0, tiled=True)
    delta_one = call(
        last_kernel, "last", shape((PAIRS, BLK, 2 * BLK), BF16), [whole()] + [anywhere()] * 2,
        stage_all, grad_input, down_half,
    )
    delta_full = lax.all_to_all(delta_one, ("y", "x", "c"), 0, 0, tiled=True)
    grad_delta = call(
        unpack_kernel, "unpack", shape((SLOTS, BLK, BLK), F32), [whole()], delta_full
    )[None]
    return down_grad, up_grad, grad_delta, grad_input


def solution(mesh):
    fine = Mesh(mesh.devices.reshape(ZH, Y, X, C, T), ALL)
    return jax.shard_map(
        per_device,
        mesh=fine,
        in_specs=(
            P(ALL, None),
            P(DP, None),
            P(DP, "t"),
            P(),
            P(None, "t"),
            P("t", None, None, None),
            P("t", None),
            P("t", None),
            P("t"),
        ),
        out_specs=(
            P(DP, None),
            P(DP, "t"),
            P("t", None, None, None),
            P(ALL, None),
        ),
        check_vma=False,
    )
```

```python
import functools

import jax
import jax.numpy as jnp
from jax import lax
from jax.experimental import pallas as pl
from jax.experimental.pallas import tpu as pltpu
from jax.sharding import Mesh, PartitionSpec as P

F32 = jnp.float32
BF16 = jnp.bfloat16
ZH, Y, X, C, T = 2, 4, 4, 2, 4
XY = Y * X
DP = ("zh", "y", "x", "c")
ALL = DP + ("t",)
BLK = 64
TOK = 128
SLOTS = 64
PAIRS = SLOTS // 2
LANES_OVER = (((1,), (1,)), ((), ()))
MIB = 1024 * 1024


GUESS = {"delta_last": 0.0, "delta_most": 0.0, "low": 10.0, "grad_input": 0.0, "stage": 0.0, "pack": 0.0, "values": 20.0, "gate": 12.0}


def whole():
    return pl.BlockSpec(memory_space=pltpu.VMEM)


def scalars():
    return pl.BlockSpec(memory_space=pltpu.SMEM)


def anywhere():
    return pl.BlockSpec(memory_space=pl.ANY)


def aligned(index, size):
    return pl.ds(pl.multiple_of(index * size, size), size)


def turn_kernel(x_hbm, after_ref, out_ref, x_ref, sems):
    step = x_ref.shape[1] // 8
    copies = []
    for i in range(8):
        at = pl.ds(i * step, step)
        copies.append(pltpu.make_async_copy(x_hbm.at[:, at], x_ref.at[:, at], sems.at[i]))
    for copy in copies:
        copy.start()
    for i in range(8):
        copies[i].wait()
        for j in range(i * step, i * step + step, 128):
            out_ref[j : j + 128, :] = x_ref[:, j : j + 128].T


def front_kernel(place, count, *refs):
    from_hbm, lows, pieces = refs[:4], refs[4 : 4 + T], refs[4 + T : 4 + 2 * T]
    grad_ref, up_ref, rows_ref, cols_ref, low_ref, sems = refs[4 + 2 * T :]
    copies = [
        pltpu.make_async_copy(there, here, sems.at[i])
        for i, (there, here) in enumerate(zip(from_hbm, (grad_ref, up_ref, rows_ref, cols_ref)))
    ]
    for copy in copies:
        copy.start()
    copies[0].wait()
    gives = []
    for k in range(T):
        at = pl.ds(pl.multiple_of((place[4] ^ k) * TOK, TOK), TOK)
        gives.append(pltpu.make_async_copy(grad_ref.at[at], pieces[k], sems.at[4 + k]))
    for give in gives:
        give.start()
    for copy in copies[1:]:
        copy.wait()
    low_ref[...] = lax.dot_general(
        grad_ref[...], up_ref[...], LANES_OVER, preferred_element_type=F32
    ).astype(BF16)
    line = jnp.concatenate(
        [rows_ref[...], cols_ref[...], jnp.full((1, 2 * SLOTS), count[0], jnp.int32)], axis=1
    ).astype(F32)
    line = jnp.broadcast_to(line, (16, line.shape[1])).astype(BF16)
    for k in range(T):
        lows[k][:TOK] = low_ref[aligned(place[4] ^ k, TOK), :]
        lows[k][TOK:] = line
    for give in gives:
        give.wait()


def up_kernel(place, grad_hbm, acts_hbm, keep_ref, give_ref, grad_ref, acts_ref, sems):
    copies = [
        pltpu.make_async_copy(acts_hbm, acts_ref, sems.at[0]),
        pltpu.make_async_copy(grad_hbm, grad_ref, sems.at[1]),
    ]
    for copy in copies:
        copy.start()
    copies[0].wait()
    rank = acts_ref.shape[1]
    half = rank // C
    here = lax.broadcasted_iota(jnp.int32, (rank, rank), 1)
    core, yx, zh = (here >> 7) ^ place[0], (here >> 3) & (XY - 1), (here >> 2) & 1
    order = lax.broadcasted_iota(jnp.int32, (rank, rank), 0) == (
        (((zh * XY + yx) * C + core) << 2) + (here & 3)
    )
    order = jnp.where(order, 1.0, 0.0).astype(BF16)
    acts = jnp.dot(acts_ref[...], order, preferred_element_type=F32).astype(BF16)
    copies[1].wait()
    step = 512

    def columns(i, carry):
        part = lax.dot_general(
            acts, grad_ref[:, aligned(i, step)], (((0,), (0,)), ((), ())),
            preferred_element_type=F32,
        )
        keep_ref[:, aligned(i, step)] = part[:half]
        give_ref[:, aligned(i, step)] = part[half:].astype(BF16)
        return carry

    lax.fori_loop(0, grad_ref.shape[1] // step, columns, 0, unroll=2)


def low_kernel(*refs):
    low_ref, table_ref = refs[-2:]
    total = refs[0][:TOK].astype(F32)
    for piece in refs[1:T]:
        total += piece[:TOK].astype(F32)
    low_ref[...] = total.astype(BF16)
    for k in range(T):
        table_ref[k * 8 : k * 8 + 8] = refs[k][TOK:].astype(F32).astype(jnp.int32)[:8]


def pass_kernel(*refs):
    pass


def pack_kernel(values_ref, out_ref):
    def one(p, carry):
        out_ref[p] = jnp.concatenate([values_ref[p], values_ref[p + PAIRS]], axis=1)
        return carry

    lax.fori_loop(0, PAIRS, one, 0, unroll=4)


def down_sum_kernel(place, down_ref, keep_ref, give_ref, up_keep_ref, up_give_ref):
    def total(at):
        part = down_ref[0, at, :].astype(F32)
        for i in range(1, XY):
            part += down_ref[i, at, :].astype(F32)
        return part

    zh = place[5]
    keep_ref[...] = total(aligned(zh, 128))
    give_ref[...] = total(aligned(1 - zh, 128)).astype(BF16)
    up = total(slice(256, None))
    rank = up.shape[1]
    for j in range(up.shape[0] // 8):
        low, high = up[j * 8 : j * 8 + 4], up[j * 8 + 4 : j * 8 + 8]
        at = slice(j * rank, (j + 1) * rank)
        up_keep_ref[:, at] = jnp.where(zh == 0, low, high)
        up_give_ref[:, at] = jnp.where(zh == 0, high, low)


def down_half_kernel(keep_ref, far_ref, out_ref):
    out_ref[...] = (keep_ref[...] + far_ref[...].astype(F32)).astype(BF16)


def down_last_kernel(*refs):
    total = refs[0][...].astype(F32)
    for part in refs[1:T]:
        total += part[...].astype(F32)
    refs[-1][...] = total


def stage_kernel(place, delta_ref, *refs):
    out_ref, sum_ref = refs[-2:]
    for k in range(T):
        total = delta_ref[0, k].astype(F32)
        for i in range(1, XY):
            total += delta_ref[i, k].astype(F32)
        sum_ref[k] = total
    for t in range(T):
        part = sum_ref[place[4] ^ t].astype(BF16)
        for zh in range(ZH):
            out_ref[zh * T + t] = part


def last_kernel(parts_ref, after_ref, after_too_ref, delta_ref):
    total = parts_ref[0].astype(F32)
    for i in range(1, ZH * T):
        total += parts_ref[i].astype(F32)
    delta = total.astype(BF16)
    for p in range(PAIRS):
        delta_ref[p] = delta


def unpack_kernel(pairs_ref, out_ref):
    def one(p, carry):
        pair = pairs_ref[p].astype(F32)
        out_ref[p] = pair[:, :BLK]
        out_ref[p + PAIRS] = pair[:, BLK:]
        return carry

    lax.fori_loop(0, PAIRS, one, 0, unroll=4)


def down_kernel(
    place, xt_ref, xt_far_ref, low_ref, low_far_ref, up_ref, up_far_ref, out_hbm, out_ref, sems
):
    low, low_far = low_ref[...], low_far_ref[...]
    core = place[0]
    rank = low.shape[1]
    copies = []
    for i in range(XY):
        for zh in range(ZH):
            at = aligned((zh * XY + i) * C + core, 128)
            total = jnp.dot(xt_ref[at, :], low, preferred_element_type=F32)
            total += jnp.dot(xt_far_ref[at, :], low_far, preferred_element_type=F32)
            out_ref[i, zh * 128 : (zh + 1) * 128] = total.astype(BF16)
        if i % 2 == 0:
            at = slice(i * 8, i * 8 + 16)
            up = up_ref[at, :] + up_far_ref[at, :].astype(F32)
        mine = up[i % 2 * 8 : i % 2 * 8 + 8]
        for j in range(0, mine.shape[1] // rank, 2):
            two = [mine[:, (j + n) * rank : (j + n + 1) * rank] for n in range(2)]
            out_ref[i, 256 + j * 8 : 256 + j * 8 + 16] = jnp.concatenate(two, axis=0).astype(BF16)
        copies.append(pltpu.make_async_copy(out_ref.at[i], out_hbm.at[i], sems.at[i]))
        copies[-1].start()
    for copy in copies:
        copy.wait()


def delta_kernel(pieces, place, table, xt_ref, xt_far_ref, *refs):
    n = len(pieces)
    near, far = refs[:n], refs[n : 2 * n]
    all_ref, grad_ref, out_ref, gt_ref, both_ref, sems = refs[-6:]
    width = near[0].shape[1]
    core = place[0]
    for j in range(n):

        def turn(i, carry, j=j):
            at = pl.ds(pl.multiple_of(i * 128, 128), 128)
            own = near[j][:, at].T
            both_ref[at, j * 256 : j * 256 + 128] = own
            both_ref[at, j * 256 + 128 : j * 256 + 256] = far[j][:, at].T
            gt_ref[pl.ds(pl.multiple_of(j * width + i * 128, 128), 128), :] = own
            return carry

        lax.fori_loop(0, width // 128, turn, 0, unroll=4)
    keep = pltpu.make_async_copy(gt_ref, grad_ref, sems.at[0])
    keep.start()

    lane = lax.broadcasted_iota(jnp.int32, (BLK, 2 * BLK), 1)

    def rows_of(index):
        return jnp.concatenate(
            [xt_ref[aligned(index, BLK), :], xt_far_ref[aligned(index, BLK), :]], axis=1
        )

    def pair(i, carry):
        s0 = i * C + core
        s1 = s0 + PAIRS
        for j, k in enumerate(pieces):
            xt = jnp.concatenate([rows_of(table[8 * k, s0]), rows_of(table[8 * k, s1])], axis=0)
            gt = jnp.concatenate(
                [
                    both_ref[aligned(table[8 * k, SLOTS + s], BLK), j * 256 : j * 256 + 256]
                    for s in (s0, s1)
                ],
                axis=0,
            )
            full = lax.dot_general(xt, gt, LANES_OVER, preferred_element_type=F32)
            live = jnp.where(lane < BLK, s0, s1) < table[8 * k, 2 * SLOTS]
            both = jnp.where(lane < BLK, full[:BLK], full[BLK:])
            out_ref[i, j] = jnp.where(live, both, 0.0).astype(BF16)
        return carry

    lax.fori_loop(0, XY, pair, 0, unroll=4)
    give = pltpu.make_async_copy(out_ref, all_ref.at[:, pieces[0] : pieces[0] + n], sems.at[1])
    give.start()
    keep.wait()
    give.wait()


def input_kernel(place, table, low_ref, *refs):
    from_hbm = refs[:7]
    out_hbm, acc_ref, down_ref, gt_ref, values, out_ref, sems = refs[7:]
    most = from_hbm[1].shape[0]
    to_vmem = (
        down_ref, gt_ref.at[:most], gt_ref.at[most:], values.at[0], values.at[1], values.at[2], values.at[3],
    )
    copies = [
        pltpu.make_async_copy(there, here, sems.at[n])
        for n, (there, here) in enumerate(zip(from_hbm, to_vmem))
    ]
    for copy in copies:
        copy.start()
    low = low_ref[...]
    step = 512
    width = gt_ref.shape[0] // T

    def dense(i, carry):
        acc_ref[aligned(i, step), :] = lax.dot_general(
            down_ref[aligned(i, step), :], low, LANES_OVER, preferred_element_type=F32
        )
        return carry

    copies[0].wait()
    lax.fori_loop(0, acc_ref.shape[0] // step, dense, 0, unroll=2)
    for copy in copies[1:]:
        copy.wait()
    lane = lax.broadcasted_iota(jnp.int32, (BLK, 2 * BLK), 1)

    def product(v, k, s0, s1):
        zero = jnp.zeros_like(v)
        live = table[8 * k, 2 * SLOTS]
        top = jnp.where((lane < BLK) & (s0 < live), v, zero)
        bottom = jnp.where((lane >= BLK) & (s1 < live), v, zero)
        gt = jnp.concatenate(
            [
                gt_ref[aligned(table[8 * k, SLOTS + s] + k * (width // BLK), BLK), :]
                for s in (s0, s1)
            ],
            axis=0,
        )
        return jnp.dot(jnp.concatenate([top, bottom], axis=0), gt, preferred_element_type=F32)

    def pair(i, carry):
        done = []
        for s0 in (2 * i, 2 * i + 1):
            s1 = s0 + PAIRS
            for m in range(T):
                k = 0 if m == 0 else place[m]
                done.append((k, s0, s1, product(values[m, s0], k, s0, s1)))
        for k, s0, s1, part in done:
            for s, add in ((s0, part[:BLK]), (s1, part[BLK:])):
                at = aligned(table[8 * k, s], BLK)
                acc_ref[at, :] = acc_ref[at, :] + add
        return carry

    lax.fori_loop(0, PAIRS // 2, pair, 0)

    gives = []
    step = 1024
    for j in range(0, out_ref.shape[1], step):
        for i in range(j, j + step, 128):
            out_ref[:, i : i + 128] = acc_ref[i : i + 128, :].T.astype(BF16)
        at = pl.ds(j, step)
        gives.append(
            pltpu.make_async_copy(out_ref.at[:, at], out_hbm.at[:, at], sems.at[7 + j // step])
        )
        gives[-1].start()
    for give in gives:
        give.wait()


def ring(shift_of_core):
    def place(z, c):
        return (z // T * C + c) * T + z % T

    n = ZH * T
    return [
        (place(z, c), place((z + shift_of_core[c]) % n, c)) for z in range(n) for c in range(C)
    ]


def swap(array, axis="c"):
    return lax.ppermute(array, axis, [(0, 1), (1, 0)])


def cross(array, k):
    return lax.ppermute(array, "t", [(i, i ^ k) for i in range(T)])


def call(kernel, name, outs, in_specs, *args, out_specs=None, scratch=(), room=16, **grid):
    return pl.pallas_call(
        kernel,
        out_shape=outs,
        in_specs=in_specs,
        out_specs=out_specs if out_specs is not None else jax.tree.map(lambda _: whole(), outs),
        scratch_shapes=scratch,
        compiler_params=pltpu.CompilerParams(vmem_limit_bytes=room * MIB),
        cost_estimate=pl.CostEstimate(
            flops=int(GUESS.get(name, 0) * 1000000000) + 1024, bytes_accessed=1024, transcendentals=0
        ),
        name=name,
        **grid,
    )(*args)


def per_device(x_own, acts, grad, down, up, values, slot_rows, slot_cols, count):
    zh, c, t = lax.axis_index("zh"), lax.axis_index("c"), lax.axis_index("t")
    feat, width, rank = x_own.shape[1], grad.shape[1], up.shape[0]
    place = jnp.stack(
        [c, t ^ ((t - 1) % T), t ^ ((t + 1) % T), 2 + 0 * t, t, zh]
    ).astype(jnp.int32)
    rows = TOK + 16
    shape = jax.ShapeDtypeStruct

    given = call(
        front_kernel, "front",
        (shape((rows, rank), BF16),) * T + (shape((TOK, width), BF16),) * T,
        [scalars()] * 2 + [anywhere()] * 4, place, count, grad, up, slot_rows, slot_cols,
        out_specs=(whole(),) * T + (anywhere(),) * T, room=56,
        scratch=[
            pltpu.VMEM(grad.shape, BF16),
            pltpu.VMEM(up.shape, BF16),
            pltpu.VMEM((1, SLOTS), jnp.int32),
            pltpu.VMEM((1, SLOTS), jnp.int32),
            pltpu.VMEM((T * TOK, rank), BF16),
            pltpu.SemaphoreType.DMA((4 + T,)),
        ],
    )
    parts, near = given[:T], given[T:]
    parts = [parts[0]] + [cross(parts[k], k) for k in (1, 2, 3)]
    near = [near[0]] + [cross(near[k], k) for k in (1, 2, 3)]

    xt = call(
        turn_kernel, "turn_input", shape((feat, TOK), BF16),
        [anywhere()] * 2, x_own, given[0],
        scratch=[pltpu.VMEM(x_own.shape, BF16), pltpu.SemaphoreType.DMA((8,))],
    )
    xt_far = swap(xt)

    half = shape((rank // C, width), BF16)
    up_keep, up_give = call(
        up_kernel, "up_part", (shape(half.shape, F32), half), [scalars()] + [anywhere()] * 2,
        place, grad, acts,
        scratch=[
            pltpu.VMEM(grad.shape, BF16),
            pltpu.VMEM(acts.shape, BF16),
            pltpu.SemaphoreType.DMA((2,)),
        ],
    )
    up_got = swap(up_give)

    low, table = call(
        low_kernel, "low", (shape((TOK, rank), BF16), shape((8 * T, rank), jnp.int32)),
        [whole()] * T + [anywhere()], *parts, up_give,
    )
    low_far = swap(low)

    size = XY, ZH * 128 + ZH * 4 * width // rank, rank
    down_part = call(
        down_kernel, "down_part", shape(size, BF16), [scalars()] + [whole()] * 6,
        place, xt, xt_far, low, low_far, up_keep, up_got,
        out_specs=anywhere(),
        scratch=[pltpu.VMEM(size, BF16), pltpu.SemaphoreType.DMA((XY,))],
    )
    down_all = lax.all_to_all(down_part, ("y", "x"), 0, 0, tiled=True)
    down_keep, down_give, up_sum, up_give = call(
        down_sum_kernel, "down_sum",
        (shape((128, rank), F32), shape((128, rank), BF16)) + (shape((4, width), F32),) * 2,
        [scalars(), whole()], place, down_all,
    )
    up_grad = up_sum + swap(up_give, "zh")
    down_half = call(
        down_half_kernel, "down_half", shape((128, rank), BF16), [whole()] * 2,
        down_keep, swap(down_give, "zh"),
    )
    down_grad = call(
        down_last_kernel, "down_last", shape((128, rank), F32), [whole()] * T,
        down_half, *[cross(down_half, k) for k in (1, 2, 3)],
    )

    def delta_call(pieces, *before):
        n = len(pieces)
        return call(
            functools.partial(delta_kernel, pieces), "delta_last" if before else "delta_most",
            (shape((XY, T, BLK, 2 * BLK), BF16), shape((n * width, TOK), BF16)),
            [scalars()] * 2 + [whole()] * (2 + 2 * n) + [anywhere()] * len(before),
            place, table, xt, xt_far, *[near[k] for k in pieces], *[far[k] for k in pieces],
            *before,
            out_specs=(anywhere(), anywhere()), room=24,
            scratch=[
                pltpu.VMEM((XY, n, BLK, 2 * BLK), BF16),
                pltpu.VMEM((n * width, TOK), BF16),
                pltpu.VMEM((width, 256 * n), BF16),
                pltpu.SemaphoreType.DMA((2,)),
            ],
            input_output_aliases={4 + 2 * n: 0} if before else {},
        )

    far = [swap(near[k]) for k in (0, 1, 2)]
    delta_most, grad_most = delta_call((0, 1, 2))
    near[3] = call(
        pass_kernel, "gate", shape((TOK, width), BF16), [anywhere()] * 2, near[3], delta_most,
        out_specs=anywhere(), input_output_aliases={0: 0},
    )
    far.append(swap(near[3]))
    delta_full, grad_last = delta_call((3,), delta_most)
    delta_part = call(
        pass_kernel, "join", shape((XY, T, BLK, 2 * BLK), BF16), [anywhere()] * 2,
        delta_full, down_all,
        out_specs=anywhere(), input_output_aliases={0: 0},
    )
    delta_all = lax.all_to_all(delta_part, ("y", "x"), 0, 0, tiled=True)

    packed = call(
        pack_kernel, "pack", shape((PAIRS, BLK, 2 * BLK), BF16), [whole()], values[0],
    )
    axes = ("zh", "t")
    got = [
        lax.ppermute(packed, axes, [(i, (i + 1) % (ZH * T)) for i in range(ZH * T)]),
        lax.ppermute(packed, axes, [(i, (i - 1) % (ZH * T)) for i in range(ZH * T)]),
        lax.ppermute(packed, ("zh", "c", "t"), ring((2, -2))),
    ]
    got = call(
        pass_kernel, "values", (shape(packed.shape, BF16),) * 3, [anywhere()] * 3, *got,
        out_specs=(anywhere(),) * 3, input_output_aliases={0: 0, 1: 1, 2: 2},
    )
    grad_input = call(
        input_kernel, "grad_input", shape((TOK, feat), BF16),
        [scalars()] * 2 + [whole()] + [anywhere()] * 7,
        place, table, low, down, grad_most, grad_last, packed, *got, room=56,
        out_specs=anywhere(),
        scratch=[
            pltpu.VMEM((feat, TOK), F32),
            pltpu.VMEM(down.shape, BF16),
            pltpu.VMEM((T * width, TOK), BF16),
            pltpu.VMEM((T, PAIRS, BLK, 2 * BLK), BF16),
            pltpu.VMEM((TOK, feat), BF16),
            pltpu.SemaphoreType.DMA((7 + feat // 1024,)),
        ],
    )

    stage = call(
        stage_kernel, "stage", shape((ZH * T, BLK, 128), BF16),
        [scalars(), whole()] + [anywhere()] * 2, place, delta_all, down_half, got[0],
        scratch=[pltpu.VMEM((T, BLK, 2 * BLK), F32)],
    )
    stage_all = lax.all_to_all(stage, ("zh", "t"), 0, 0, tiled=True)
    delta_one = call(
        last_kernel, "last", shape((PAIRS, BLK, 2 * BLK), BF16), [whole()] + [anywhere()] * 2,
        stage_all, down_grad, up_grad,
    )
    delta_full = lax.all_to_all(delta_one, ("y", "x", "c"), 0, 0, tiled=True)
    grad_delta = call(
        unpack_kernel, "unpack", shape((SLOTS, BLK, BLK), F32), [whole()], delta_full
    )[None]
    return down_grad, up_grad, grad_delta, grad_input


def solution(mesh):
    fine = Mesh(mesh.devices.reshape(ZH, Y, X, C, T), ALL)
    return jax.shard_map(
        per_device,
        mesh=fine,
        in_specs=(
            P(ALL, None),
            P(DP, None),
            P(DP, "t"),
            P(),
            P(None, "t"),
            P("t", None, None, None),
            P("t", None),
            P("t", None),
            P("t"),
        ),
        out_specs=(
            P(DP, None),
            P(DP, "t"),
            P("t", None, None, None),
            P(ALL, None),
        ),
        check_vma=False,
    )
```

```python
import functools

import jax
import jax.numpy as jnp
from jax import lax
from jax.experimental import pallas as pl
from jax.experimental.pallas import tpu as pltpu
from jax.sharding import Mesh, PartitionSpec as P

F32 = jnp.float32
BF16 = jnp.bfloat16
ZH, Y, X, C, T = 2, 4, 4, 2, 4
XY = Y * X
DP = ("zh", "y", "x", "c")
ALL = DP + ("t",)
BLK = 64
TOK = 128
SLOTS = 64
PAIRS = SLOTS // 2
LANES_OVER = (((1,), (1,)), ((), ()))
MIB = 1024 * 1024


GUESS = {"delta_last": 0.0, "delta_most": 0.0, "low": 10.0, "grad_input": 0.0, "stage": 0.0, "pack": 0.0, "values": 20.0, "gate": 12.0}


def whole():
    return pl.BlockSpec(memory_space=pltpu.VMEM)


def scalars():
    return pl.BlockSpec(memory_space=pltpu.SMEM)


def anywhere():
    return pl.BlockSpec(memory_space=pl.ANY)


def aligned(index, size):
    return pl.ds(pl.multiple_of(index * size, size), size)


def turn_kernel(x_hbm, after_ref, out_ref, x_ref, sems):
    step = x_ref.shape[1] // 8
    copies = []
    for i in range(8):
        at = pl.ds(i * step, step)
        copies.append(pltpu.make_async_copy(x_hbm.at[:, at], x_ref.at[:, at], sems.at[i]))
    for copy in copies:
        copy.start()
    for i in range(8):
        copies[i].wait()
        for j in range(i * step, i * step + step, 128):
            out_ref[j : j + 128, :] = x_ref[:, j : j + 128].T


def front_kernel(place, count, *refs):
    from_hbm, lows, pieces = refs[:4], refs[4 : 4 + T], refs[4 + T : 4 + 2 * T]
    grad_ref, up_ref, rows_ref, cols_ref, low_ref, sems = refs[4 + 2 * T :]
    copies = [
        pltpu.make_async_copy(there, here, sems.at[i])
        for i, (there, here) in enumerate(zip(from_hbm, (grad_ref, up_ref, rows_ref, cols_ref)))
    ]
    for copy in copies:
        copy.start()
    copies[0].wait()
    gives = []
    for k in range(T):
        at = pl.ds(pl.multiple_of((place[4] ^ k) * TOK, TOK), TOK)
        gives.append(pltpu.make_async_copy(grad_ref.at[at], pieces[k], sems.at[4 + k]))
    for give in gives:
        give.start()
    for copy in copies[1:]:
        copy.wait()
    low_ref[...] = lax.dot_general(
        grad_ref[...], up_ref[...], LANES_OVER, preferred_element_type=F32
    ).astype(BF16)
    line = jnp.concatenate(
        [rows_ref[...], cols_ref[...], jnp.full((1, 2 * SLOTS), count[0], jnp.int32)], axis=1
    ).astype(F32)
    line = jnp.broadcast_to(line, (16, line.shape[1])).astype(BF16)
    for k in range(T):
        lows[k][:TOK] = low_ref[aligned(place[4] ^ k, TOK), :]
        lows[k][TOK:] = line
    for give in gives:
        give.wait()


def up_kernel(place, grad_hbm, acts_hbm, keep_ref, give_ref, grad_ref, acts_ref, sems):
    copies = [
        pltpu.make_async_copy(acts_hbm, acts_ref, sems.at[0]),
        pltpu.make_async_copy(grad_hbm, grad_ref, sems.at[1]),
    ]
    for copy in copies:
        copy.start()
    copies[0].wait()
    rank = acts_ref.shape[1]
    half = rank // C
    here = lax.broadcasted_iota(jnp.int32, (rank, rank), 1)
    core, yx, zh = (here >> 7) ^ place[0], (here >> 3) & (XY - 1), (here >> 2) & 1
    order = lax.broadcasted_iota(jnp.int32, (rank, rank), 0) == (
        (((zh * XY + yx) * C + core) << 2) + (here & 3)
    )
    order = jnp.where(order, 1.0, 0.0).astype(BF16)
    acts = jnp.dot(acts_ref[...], order, preferred_element_type=F32).astype(BF16)
    copies[1].wait()
    step = 512

    def columns(i, carry):
        part = lax.dot_general(
            acts, grad_ref[:, aligned(i, step)], (((0,), (0,)), ((), ())),
            preferred_element_type=F32,
        )
        keep_ref[:, aligned(i, step)] = part[:half]
        give_ref[:, aligned(i, step)] = part[half:].astype(BF16)
        return carry

    lax.fori_loop(0, grad_ref.shape[1] // step, columns, 0, unroll=2)


def low_kernel(*refs):
    low_ref, table_ref = refs[-2:]
    total = refs[0][:TOK].astype(F32)
    for piece in refs[1:T]:
        total += piece[:TOK].astype(F32)
    low_ref[...] = total.astype(BF16)
    for k in range(T):
        table_ref[k * 8 : k * 8 + 8] = refs[k][TOK:].astype(F32).astype(jnp.int32)[:8]


def pass_kernel(*refs):
    pass


def pack_kernel(values_ref, out_ref):
    def one(p, carry):
        out_ref[p] = jnp.concatenate([values_ref[p], values_ref[p + PAIRS]], axis=1)
        return carry

    lax.fori_loop(0, PAIRS, one, 0, unroll=4)


def down_sum_kernel(place, down_ref, keep_ref, give_ref, up_ref):
    def total(at):
        part = down_ref[0, at, :].astype(F32)
        for i in range(1, XY):
            part += down_ref[i, at, :].astype(F32)
        return part

    zh = place[5]
    keep_ref[...] = total(aligned(zh, 128))
    give_ref[:128] = total(aligned(1 - zh, 128)).astype(BF16)
    up = total(slice(256, None))
    rank = up.shape[1]
    give = []
    for j in range(up.shape[0] // 8):
        low, high = up[j * 8 : j * 8 + 4], up[j * 8 + 4 : j * 8 + 8]
        up_ref[:, j * rank : (j + 1) * rank] = jnp.where(zh == 0, low, high)
        give.append(jnp.where(zh == 0, high, low))
    give_ref[128:] = jnp.concatenate(give, axis=0).astype(BF16)


def down_half_kernel(keep_ref, far_ref, up_ref, out_ref, up_out_ref):
    out_ref[...] = (keep_ref[...] + far_ref[:128].astype(F32)).astype(BF16)
    up = far_ref[128:].astype(F32)
    rank = up.shape[1]
    for j in range(up.shape[0] // 4):
        at = slice(j * rank, (j + 1) * rank)
        up_out_ref[:, at] = up_ref[:, at] + up[j * 4 : j * 4 + 4]


def down_last_kernel(*refs):
    total = refs[0][...].astype(F32)
    for part in refs[1:T]:
        total += part[...].astype(F32)
    refs[-1][...] = total


def stage_kernel(place, delta_ref, *refs):
    out_ref, sum_ref = refs[-2:]
    for k in range(T):
        total = delta_ref[0, k].astype(F32)
        for i in range(1, XY):
            total += delta_ref[i, k].astype(F32)
        sum_ref[k] = total
    for t in range(T):
        part = sum_ref[place[4] ^ t].astype(BF16)
        for zh in range(ZH):
            out_ref[zh * T + t] = part


def last_kernel(parts_ref, after_ref, delta_ref):
    total = parts_ref[0].astype(F32)
    for i in range(1, ZH * T):
        total += parts_ref[i].astype(F32)
    delta = total.astype(BF16)
    for p in range(PAIRS):
        delta_ref[p] = delta


def unpack_kernel(pairs_ref, out_ref):
    def one(p, carry):
        pair = pairs_ref[p].astype(F32)
        out_ref[p] = pair[:, :BLK]
        out_ref[p + PAIRS] = pair[:, BLK:]
        return carry

    lax.fori_loop(0, PAIRS, one, 0, unroll=4)


def down_kernel(place, xt_ref, xt_far_ref, low_ref, low_far_ref, up_ref, up_far_ref, out_ref):
    low, low_far = low_ref[...], low_far_ref[...]
    core = place[0]
    rank = low.shape[1]

    def block(i, carry):
        for zh in range(ZH):
            at = aligned((zh * XY + i) * C + core, 128)
            total = jnp.dot(xt_ref[at, :], low, preferred_element_type=F32)
            total += jnp.dot(xt_far_ref[at, :], low_far, preferred_element_type=F32)
            out_ref[i, zh * 128 : (zh + 1) * 128] = total.astype(BF16)
        return carry

    lax.fori_loop(0, XY, block, 0, unroll=4)
    for i in range(0, XY, 2):
        at = slice(i * 8, i * 8 + 16)
        for j in range(0, up_ref.shape[1] // rank, 2):
            two = []
            for n in (j, j + 1):
                lanes = slice(n * rank, (n + 1) * rank)
                two.append(up_ref[at, lanes] + up_far_ref[at, lanes].astype(F32))
            for n in range(2):
                both = [part[n * 8 : n * 8 + 8] for part in two]
                out_ref[i + n, 256 + j * 8 : 256 + j * 8 + 16] = jnp.concatenate(both, 0).astype(BF16)


def delta_kernel(pieces, place, table, xt_ref, xt_far_ref, *refs):
    n = len(pieces)
    near, far = refs[:n], refs[n : 2 * n]
    all_ref, grad_ref, out_ref, gt_ref, both_ref, sems = refs[-6:]
    width = near[0].shape[1]
    core = place[0]
    for j in range(n):

        def turn(i, carry, j=j):
            at = pl.ds(pl.multiple_of(i * 128, 128), 128)
            own = near[j][:, at].T
            both_ref[at, j * 256 : j * 256 + 128] = own
            both_ref[at, j * 256 + 128 : j * 256 + 256] = far[j][:, at].T
            gt_ref[pl.ds(pl.multiple_of(j * width + i * 128, 128), 128), :] = own
            return carry

        lax.fori_loop(0, width // 128, turn, 0, unroll=4)
    keep = pltpu.make_async_copy(gt_ref, grad_ref, sems.at[0])
    keep.start()

    lane = lax.broadcasted_iota(jnp.int32, (BLK, 2 * BLK), 1)

    def rows_of(index):
        return jnp.concatenate(
            [xt_ref[aligned(index, BLK), :], xt_far_ref[aligned(index, BLK), :]], axis=1
        )

    def pair(i, carry):
        s0 = i * C + core
        s1 = s0 + PAIRS
        for j, k in enumerate(pieces):
            xt = jnp.concatenate([rows_of(table[8 * k, s0]), rows_of(table[8 * k, s1])], axis=0)
            gt = jnp.concatenate(
                [
                    both_ref[aligned(table[8 * k, SLOTS + s], BLK), j * 256 : j * 256 + 256]
                    for s in (s0, s1)
                ],
                axis=0,
            )
            full = lax.dot_general(xt, gt, LANES_OVER, preferred_element_type=F32)
            live = jnp.where(lane < BLK, s0, s1) < table[8 * k, 2 * SLOTS]
            both = jnp.where(lane < BLK, full[:BLK], full[BLK:])
            out_ref[i, j] = jnp.where(live, both, 0.0).astype(BF16)
        return carry

    lax.fori_loop(0, XY, pair, 0, unroll=4)
    give = pltpu.make_async_copy(out_ref, all_ref.at[:, pieces[0] : pieces[0] + n], sems.at[1])
    give.start()
    keep.wait()
    give.wait()


def input_kernel(place, table, low_ref, *refs):
    from_hbm = refs[:7]
    out_hbm, acc_ref, down_ref, gt_ref, values, out_ref, sems = refs[7:]
    most = from_hbm[1].shape[0]
    to_vmem = (
        down_ref, gt_ref.at[:most], gt_ref.at[most:], values.at[0], values.at[1], values.at[2], values.at[3],
    )
    copies = [
        pltpu.make_async_copy(there, here, sems.at[n])
        for n, (there, here) in enumerate(zip(from_hbm, to_vmem))
    ]
    for copy in copies:
        copy.start()
    low = low_ref[...]
    step = 512
    width = gt_ref.shape[0] // T

    def dense(i, carry):
        acc_ref[aligned(i, step), :] = lax.dot_general(
            down_ref[aligned(i, step), :], low, LANES_OVER, preferred_element_type=F32
        )
        return carry

    copies[0].wait()
    lax.fori_loop(0, acc_ref.shape[0] // step, dense, 0, unroll=2)
    for copy in copies[1:]:
        copy.wait()
    lane = lax.broadcasted_iota(jnp.int32, (BLK, 2 * BLK), 1)

    def product(v, k, s0, s1):
        zero = jnp.zeros_like(v)
        live = table[8 * k, 2 * SLOTS]
        top = jnp.where((lane < BLK) & (s0 < live), v, zero)
        bottom = jnp.where((lane >= BLK) & (s1 < live), v, zero)
        gt = jnp.concatenate(
            [
                gt_ref[aligned(table[8 * k, SLOTS + s] + k * (width // BLK), BLK), :]
                for s in (s0, s1)
            ],
            axis=0,
        )
        return jnp.dot(jnp.concatenate([top, bottom], axis=0), gt, preferred_element_type=F32)

    def pair(i, carry):
        done = []
        for s0 in (2 * i, 2 * i + 1):
            s1 = s0 + PAIRS
            for m in range(T):
                k = 0 if m == 0 else place[m]
                done.append((k, s0, s1, product(values[m, s0], k, s0, s1)))
        for k, s0, s1, part in done:
            for s, add in ((s0, part[:BLK]), (s1, part[BLK:])):
                at = aligned(table[8 * k, s], BLK)
                acc_ref[at, :] = acc_ref[at, :] + add
        return carry

    lax.fori_loop(0, PAIRS // 2, pair, 0)

    gives = []
    step = 1024
    for j in range(0, out_ref.shape[1], step):
        for i in range(j, j + step, 128):
            out_ref[:, i : i + 128] = acc_ref[i : i + 128, :].T.astype(BF16)
        at = pl.ds(j, step)
        gives.append(
            pltpu.make_async_copy(out_ref.at[:, at], out_hbm.at[:, at], sems.at[7 + j // step])
        )
        gives[-1].start()
    for give in gives:
        give.wait()


def ring(shift_of_core):
    def place(z, c):
        return (z // T * C + c) * T + z % T

    n = ZH * T
    return [
        (place(z, c), place((z + shift_of_core[c]) % n, c)) for z in range(n) for c in range(C)
    ]


def swap(array, axis="c"):
    return lax.ppermute(array, axis, [(0, 1), (1, 0)])


def cross(array, k):
    return lax.ppermute(array, "t", [(i, i ^ k) for i in range(T)])


def call(kernel, name, outs, in_specs, *args, out_specs=None, scratch=(), room=16, **grid):
    return pl.pallas_call(
        kernel,
        out_shape=outs,
        in_specs=in_specs,
        out_specs=out_specs if out_specs is not None else jax.tree.map(lambda _: whole(), outs),
        scratch_shapes=scratch,
        compiler_params=pltpu.CompilerParams(vmem_limit_bytes=room * MIB),
        cost_estimate=pl.CostEstimate(
            flops=int(GUESS.get(name, 0) * 1000000000) + 1024, bytes_accessed=1024, transcendentals=0
        ),
        name=name,
        **grid,
    )(*args)


def per_device(x_own, acts, grad, down, up, values, slot_rows, slot_cols, count):
    zh, c, t = lax.axis_index("zh"), lax.axis_index("c"), lax.axis_index("t")
    feat, width, rank = x_own.shape[1], grad.shape[1], up.shape[0]
    place = jnp.stack(
        [c, t ^ ((t - 1) % T), t ^ ((t + 1) % T), 2 + 0 * t, t, zh]
    ).astype(jnp.int32)
    rows = TOK + 16
    shape = jax.ShapeDtypeStruct

    given = call(
        front_kernel, "front",
        (shape((rows, rank), BF16),) * T + (shape((TOK, width), BF16),) * T,
        [scalars()] * 2 + [anywhere()] * 4, place, count, grad, up, slot_rows, slot_cols,
        out_specs=(whole(),) * T + (anywhere(),) * T, room=56,
        scratch=[
            pltpu.VMEM(grad.shape, BF16),
            pltpu.VMEM(up.shape, BF16),
            pltpu.VMEM((1, SLOTS), jnp.int32),
            pltpu.VMEM((1, SLOTS), jnp.int32),
            pltpu.VMEM((T * TOK, rank), BF16),
            pltpu.SemaphoreType.DMA((4 + T,)),
        ],
    )
    parts, near = given[:T], given[T:]
    parts = [parts[0]] + [cross(parts[k], k) for k in (1, 2, 3)]
    near = [near[0]] + [cross(near[k], k) for k in (1, 2, 3)]

    xt = call(
        turn_kernel, "turn_input", shape((feat, TOK), BF16),
        [anywhere()] * 2, x_own, given[T],
        scratch=[pltpu.VMEM(x_own.shape, BF16), pltpu.SemaphoreType.DMA((8,))],
    )
    xt_far = swap(xt)

    half = shape((rank // C, width), BF16)
    up_keep, up_give = call(
        up_kernel, "up_part", (shape(half.shape, F32), half), [scalars()] + [anywhere()] * 2,
        place, grad, acts,
        scratch=[
            pltpu.VMEM(grad.shape, BF16),
            pltpu.VMEM(acts.shape, BF16),
            pltpu.SemaphoreType.DMA((2,)),
        ],
    )
    up_got = swap(up_give)

    low, table = call(
        low_kernel, "low", (shape((TOK, rank), BF16), shape((8 * T, rank), jnp.int32)),
        [whole()] * T + [anywhere()], *parts, up_give,
    )
    low_far = swap(low)

    size = XY, ZH * 128 + ZH * 4 * width // rank, rank
    down_part = call(
        down_kernel, "down_part", shape(size, BF16), [scalars()] + [whole()] * 6,
        place, xt, xt_far, low, low_far, up_keep, up_got,
    )
    down_all = lax.all_to_all(down_part, ("y", "x"), 0, 0, tiled=True)
    down_keep, down_give, up_sum = call(
        down_sum_kernel, "down_sum",
        (
            shape((128, rank), F32),
            shape((128 + 4 * width // rank, rank), BF16),
            shape((4, width), F32),
        ),
        [scalars(), whole()], place, down_all,
    )
    down_half, up_grad = call(
        down_half_kernel, "down_half", (shape((128, rank), BF16), shape((4, width), F32)),
        [whole()] * 3, down_keep, swap(down_give, "zh"), up_sum,
    )
    down_grad = call(
        down_last_kernel, "down_last", shape((128, rank), F32), [whole()] * T,
        down_half, *[cross(down_half, k) for k in (1, 2, 3)],
    )

    def delta_call(pieces, *before):
        n = len(pieces)
        return call(
            functools.partial(delta_kernel, pieces), "delta_last" if before else "delta_most",
            (shape((XY, T, BLK, 2 * BLK), BF16), shape((n * width, TOK), BF16)),
            [scalars()] * 2 + [whole()] * (2 + 2 * n) + [anywhere()] * len(before),
            place, table, xt, xt_far, *[near[k] for k in pieces], *[far[k] for k in pieces],
            *before,
            out_specs=(anywhere(), anywhere()), room=24,
            scratch=[
                pltpu.VMEM((XY, n, BLK, 2 * BLK), BF16),
                pltpu.VMEM((n * width, TOK), BF16),
                pltpu.VMEM((width, 256 * n), BF16),
                pltpu.SemaphoreType.DMA((2,)),
            ],
            input_output_aliases={4 + 2 * n: 0} if before else {},
        )

    far = [swap(near[k]) for k in (0, 1, 2)]
    delta_most, grad_most = delta_call((0, 1, 2))
    near[3] = call(
        pass_kernel, "gate", shape((TOK, width), BF16), [anywhere()] * 2, near[3], delta_most,
        out_specs=anywhere(), input_output_aliases={0: 0},
    )
    far.append(swap(near[3]))
    delta_full, grad_last = delta_call((3,), delta_most)
    delta_part = call(
        pass_kernel, "join", shape((XY, T, BLK, 2 * BLK), BF16), [anywhere()] * 2,
        delta_full, down_all,
        out_specs=anywhere(), input_output_aliases={0: 0},
    )
    delta_all = lax.all_to_all(delta_part, ("y", "x"), 0, 0, tiled=True)

    packed = call(
        pack_kernel, "pack", shape((PAIRS, BLK, 2 * BLK), BF16), [whole()], values[0],
    )
    axes = ("zh", "t")
    got = [
        lax.ppermute(packed, axes, [(i, (i + 1) % (ZH * T)) for i in range(ZH * T)]),
        lax.ppermute(packed, axes, [(i, (i - 1) % (ZH * T)) for i in range(ZH * T)]),
        lax.ppermute(packed, ("zh", "c", "t"), ring((2, -2))),
    ]
    got = call(
        pass_kernel, "values", (shape(packed.shape, BF16),) * 3, [anywhere()] * 3, *got,
        out_specs=(anywhere(),) * 3, input_output_aliases={0: 0, 1: 1, 2: 2},
    )
    grad_input = call(
        input_kernel, "grad_input", shape((TOK, feat), BF16),
        [scalars()] * 2 + [whole()] + [anywhere()] * 7,
        place, table, low, down, grad_most, grad_last, packed, *got, room=56,
        out_specs=anywhere(),
        scratch=[
            pltpu.VMEM((feat, TOK), F32),
            pltpu.VMEM(down.shape, BF16),
            pltpu.VMEM((T * width, TOK), BF16),
            pltpu.VMEM((T, PAIRS, BLK, 2 * BLK), BF16),
            pltpu.VMEM((TOK, feat), BF16),
            pltpu.SemaphoreType.DMA((7 + feat // 1024,)),
        ],
    )

    stage = call(
        stage_kernel, "stage", shape((ZH * T, BLK, 128), BF16),
        [scalars()] + [whole()] * 2 + [anywhere()], place, delta_all, down_half, got[0],
        scratch=[pltpu.VMEM((T, BLK, 2 * BLK), F32)],
    )

    stage_all = lax.all_to_all(stage, ("zh", "t"), 0, 0, tiled=True)
    delta_one = call(
        last_kernel, "last", shape((PAIRS, BLK, 2 * BLK), BF16), [whole()] * 2, stage_all, down_grad,
    )
    delta_full = lax.all_to_all(delta_one, ("y", "x", "c"), 0, 0, tiled=True)
    grad_delta = call(
        unpack_kernel, "unpack", shape((SLOTS, BLK, BLK), F32), [whole()], delta_full
    )[None]
    return down_grad, up_grad, grad_delta, grad_input


def solution(mesh):
    fine = Mesh(mesh.devices.reshape(ZH, Y, X, C, T), ALL)
    return jax.shard_map(
        per_device,
        mesh=fine,
        in_specs=(
            P(ALL, None),
            P(DP, None),
            P(DP, "t"),
            P(),
            P(None, "t"),
            P("t", None, None, None),
            P("t", None),
            P("t", None),
            P("t"),
        ),
        out_specs=(
            P(DP, None),
            P(DP, "t"),
            P("t", None, None, None),
            P(ALL, None),
        ),
        check_vma=False,
    )
```

```python
import functools

import jax
import jax.numpy as jnp
from jax import lax
from jax.experimental import pallas as pl
from jax.experimental.pallas import tpu as pltpu
from jax.sharding import Mesh, PartitionSpec as P

F32 = jnp.float32
BF16 = jnp.bfloat16
ZH, Y, X, C, T = 2, 4, 4, 2, 4
XY = Y * X
DP = ("zh", "y", "x", "c")
ALL = DP + ("t",)
BLK = 64
TOK = 128
SLOTS = 64
PAIRS = SLOTS // 2
LANES_OVER = (((1,), (1,)), ((), ()))
MIB = 1024 * 1024


GUESS = {"delta_last": 0.0, "delta_most": 0.0, "low": 10.0, "grad_input": 0.0, "stage": 0.0, "pack": 0.0, "values": 10.0, "gate": 12.0}


def whole():
    return pl.BlockSpec(memory_space=pltpu.VMEM)


def scalars():
    return pl.BlockSpec(memory_space=pltpu.SMEM)


def anywhere():
    return pl.BlockSpec(memory_space=pl.ANY)


def aligned(index, size):
    return pl.ds(pl.multiple_of(index * size, size), size)


def turn_kernel(x_hbm, after_ref, out_ref, x_ref, sems):
    step = x_ref.shape[1] // 8
    copies = []
    for i in range(8):
        at = pl.ds(i * step, step)
        copies.append(pltpu.make_async_copy(x_hbm.at[:, at], x_ref.at[:, at], sems.at[i]))
    for copy in copies:
        copy.start()
    for i in range(8):
        copies[i].wait()
        for j in range(i * step, i * step + step, 128):
            out_ref[j : j + 128, :] = x_ref[:, j : j + 128].T


def front_kernel(place, count, *refs):
    from_hbm, lows, pieces = refs[:4], refs[4 : 4 + T], refs[4 + T : 4 + 2 * T]
    grad_ref, up_ref, rows_ref, cols_ref, low_ref, ext_ref, sems = refs[4 + 2 * T :]
    copies = [
        pltpu.make_async_copy(there, here, sems.at[i])
        for i, (there, here) in enumerate(zip(from_hbm, (grad_ref, up_ref, rows_ref, cols_ref)))
    ]
    for copy in copies:
        copy.start()
    copies[0].wait()
    gives = []
    for k in range(T):
        at = pl.ds(pl.multiple_of((place[4] ^ k) * TOK, TOK), TOK)
        gives.append(pltpu.make_async_copy(grad_ref.at[at], pieces[k], sems.at[4 + k]))
    for give in gives:
        give.start()
    for copy in copies[1:]:
        copy.wait()
    low_ref[...] = lax.dot_general(
        grad_ref[...], up_ref[...], LANES_OVER, preferred_element_type=F32
    ).astype(BF16)
    line = jnp.concatenate(
        [rows_ref[...], cols_ref[...], jnp.full((1, 2 * SLOTS), count[0], jnp.int32)], axis=1
    ).astype(F32)
    line = jnp.broadcast_to(line, (16, line.shape[1])).astype(BF16)
    for k in range(T):
        ext_ref[k, :TOK] = low_ref[aligned(place[4] ^ k, TOK), :]
        ext_ref[k, TOK:] = line
        gives.append(pltpu.make_async_copy(ext_ref.at[k], lows[k], sems.at[4 + T + k]))
        gives[-1].start()
    for give in gives:
        give.wait()


def up_kernel(place, grad_hbm, acts_hbm, keep_ref, give_ref, grad_ref, acts_ref, sems):
    copies = [
        pltpu.make_async_copy(acts_hbm, acts_ref, sems.at[0]),
        pltpu.make_async_copy(grad_hbm, grad_ref, sems.at[1]),
    ]
    for copy in copies:
        copy.start()
    copies[0].wait()
    rank = acts_ref.shape[1]
    half = rank // C
    here = lax.broadcasted_iota(jnp.int32, (rank, rank), 1)
    core, yx, zh = (here >> 7) ^ place[0], (here >> 3) & (XY - 1), (here >> 2) & 1
    order = lax.broadcasted_iota(jnp.int32, (rank, rank), 0) == (
        (((zh * XY + yx) * C + core) << 2) + (here & 3)
    )
    order = jnp.where(order, 1.0, 0.0).astype(BF16)
    acts = jnp.dot(acts_ref[...], order, preferred_element_type=F32).astype(BF16)
    copies[1].wait()
    step = 512

    def columns(i, carry):
        part = lax.dot_general(
            acts, grad_ref[:, aligned(i, step)], (((0,), (0,)), ((), ())),
            preferred_element_type=F32,
        )
        keep_ref[:, aligned(i, step)] = part[:half]
        give_ref[:, aligned(i, step)] = part[half:].astype(BF16)
        return carry

    lax.fori_loop(0, grad_ref.shape[1] // step, columns, 0, unroll=2)


def low_kernel(*refs):
    low_ref, table_ref = refs[-2:]
    total = refs[0][:TOK].astype(F32)
    for piece in refs[1:T]:
        total += piece[:TOK].astype(F32)
    low_ref[...] = total.astype(BF16)
    for k in range(T):
        table_ref[k * 8 : k * 8 + 8] = refs[k][TOK:].astype(F32).astype(jnp.int32)[:8]


def pass_kernel(*refs):
    pass


def pack_kernel(values_ref, out_ref):
    def one(p, carry):
        out_ref[p] = jnp.concatenate([values_ref[p], values_ref[p + PAIRS]], axis=1)
        return carry

    lax.fori_loop(0, PAIRS, one, 0, unroll=4)


def down_sum_kernel(place, down_ref, keep_ref, give_ref, up_ref):
    def total(at):
        part = down_ref[0, at, :].astype(F32)
        for i in range(1, XY):
            part += down_ref[i, at, :].astype(F32)
        return part

    zh = place[5]
    keep_ref[...] = total(aligned(zh, 128))
    give_ref[:128] = total(aligned(1 - zh, 128)).astype(BF16)
    up = total(slice(256, None))
    rank = up.shape[1]
    give = []
    for j in range(up.shape[0] // 8):
        low, high = up[j * 8 : j * 8 + 4], up[j * 8 + 4 : j * 8 + 8]
        up_ref[:, j * rank : (j + 1) * rank] = jnp.where(zh == 0, low, high)
        give.append(jnp.where(zh == 0, high, low))
    give_ref[128:] = jnp.concatenate(give, axis=0).astype(BF16)


def down_half_kernel(keep_ref, far_ref, up_ref, out_ref, up_out_ref):
    out_ref[...] = (keep_ref[...] + far_ref[:128].astype(F32)).astype(BF16)
    up = far_ref[128:].astype(F32)
    rank = up.shape[1]
    for j in range(up.shape[0] // 4):
        at = slice(j * rank, (j + 1) * rank)
        up_out_ref[:, at] = up_ref[:, at] + up[j * 4 : j * 4 + 4]


def down_last_kernel(*refs):
    total = refs[0][...].astype(F32)
    for part in refs[1:T]:
        total += part[...].astype(F32)
    refs[-1][...] = total


def stage_kernel(place, delta_ref, *refs):
    out_ref, sum_ref = refs[-2:]
    for k in range(T):
        total = delta_ref[0, k].astype(F32)
        for i in range(1, XY):
            total += delta_ref[i, k].astype(F32)
        sum_ref[k] = total
    for t in range(T):
        part = sum_ref[place[4] ^ t].astype(BF16)
        for zh in range(ZH):
            out_ref[zh * T + t] = part


def last_kernel(parts_ref, after_ref, delta_ref):
    total = parts_ref[0].astype(F32)
    for i in range(1, ZH * T):
        total += parts_ref[i].astype(F32)
    delta = total.astype(BF16)
    for p in range(PAIRS):
        delta_ref[p] = delta


def unpack_kernel(pairs_ref, out_ref):
    def one(p, carry):
        pair = pairs_ref[p].astype(F32)
        out_ref[p] = pair[:, :BLK]
        out_ref[p + PAIRS] = pair[:, BLK:]
        return carry

    lax.fori_loop(0, PAIRS, one, 0, unroll=4)


def down_kernel(place, xt_ref, xt_far_ref, low_ref, low_far_ref, up_ref, up_far_ref, out_ref):
    low, low_far = low_ref[...], low_far_ref[...]
    core = place[0]
    rank = low.shape[1]

    def block(i, carry):
        for zh in range(ZH):
            at = aligned((zh * XY + i) * C + core, 128)
            total = jnp.dot(xt_ref[at, :], low, preferred_element_type=F32)
            total += jnp.dot(xt_far_ref[at, :], low_far, preferred_element_type=F32)
            out_ref[i, zh * 128 : (zh + 1) * 128] = total.astype(BF16)
        return carry

    lax.fori_loop(0, XY, block, 0, unroll=4)
    for i in range(0, XY, 2):
        at = slice(i * 8, i * 8 + 16)
        for j in range(0, up_ref.shape[1] // rank, 2):
            two = []
            for n in (j, j + 1):
                lanes = slice(n * rank, (n + 1) * rank)
                two.append(up_ref[at, lanes] + up_far_ref[at, lanes].astype(F32))
            for n in range(2):
                both = [part[n * 8 : n * 8 + 8] for part in two]
                out_ref[i + n, 256 + j * 8 : 256 + j * 8 + 16] = jnp.concatenate(both, 0).astype(BF16)


def delta_kernel(pieces, place, table, xt_ref, xt_far_ref, *refs):
    n = len(pieces)
    near, far = refs[:n], refs[n : 2 * n]
    all_ref, grad_ref, out_ref, gt_ref, both_ref, sems = refs[-6:]
    width = near[0].shape[1]
    core = place[0]
    for j in range(n):

        def turn(i, carry, j=j):
            at = pl.ds(pl.multiple_of(i * 128, 128), 128)
            own = near[j][:, at].T
            both_ref[at, j * 256 : j * 256 + 128] = own
            both_ref[at, j * 256 + 128 : j * 256 + 256] = far[j][:, at].T
            gt_ref[pl.ds(pl.multiple_of(j * width + i * 128, 128), 128), :] = own
            return carry

        lax.fori_loop(0, width // 128, turn, 0, unroll=4)
    keep = pltpu.make_async_copy(gt_ref, grad_ref, sems.at[0])
    keep.start()

    lane = lax.broadcasted_iota(jnp.int32, (BLK, 2 * BLK), 1)

    def rows_of(index):
        return jnp.concatenate(
            [xt_ref[aligned(index, BLK), :], xt_far_ref[aligned(index, BLK), :]], axis=1
        )

    def pair(i, carry):
        s0 = i * C + core
        s1 = s0 + PAIRS
        for j, k in enumerate(pieces):
            xt = jnp.concatenate([rows_of(table[8 * k, s0]), rows_of(table[8 * k, s1])], axis=0)
            gt = jnp.concatenate(
                [
                    both_ref[aligned(table[8 * k, SLOTS + s], BLK), j * 256 : j * 256 + 256]
                    for s in (s0, s1)
                ],
                axis=0,
            )
            full = lax.dot_general(xt, gt, LANES_OVER, preferred_element_type=F32)
            live = jnp.where(lane < BLK, s0, s1) < table[8 * k, 2 * SLOTS]
            both = jnp.where(lane < BLK, full[:BLK], full[BLK:])
            out_ref[i, j] = jnp.where(live, both, 0.0).astype(BF16)
        return carry

    lax.fori_loop(0, XY, pair, 0, unroll=4)
    give = pltpu.make_async_copy(out_ref, all_ref.at[:, pieces[0] : pieces[0] + n], sems.at[1])
    give.start()
    keep.wait()
    give.wait()


def spread(table, gt_ref, acc_ref, parts):
    lane = lax.broadcasted_iota(jnp.int32, (BLK, 2 * BLK), 1)
    done = []
    for v, k, base, s0, s1 in parts:
        zero = jnp.zeros_like(v)
        live = table[8 * k, 2 * SLOTS]
        top = jnp.where((lane < BLK) & (s0 < live), v, zero)
        bottom = jnp.where((lane >= BLK) & (s1 < live), v, zero)
        gt = jnp.concatenate(
            [gt_ref[aligned(table[8 * k, SLOTS + s] + base, BLK), :] for s in (s0, s1)], axis=0
        )
        both = jnp.concatenate([top, bottom], axis=0)
        done.append(jnp.dot(both, gt, preferred_element_type=F32))
    for (_, k, _, s0, s1), part in zip(parts, done):
        for s, add in ((s0, part[:BLK]), (s1, part[BLK:])):
            at = aligned(table[8 * k, s], BLK)
            acc_ref[at, :] = acc_ref[at, :] + add


def dense_kernel(table, low_ref, down_hbm, gt_hbm, own_hbm, acc_ref, token_ref, *refs):
    down_ref, gt_ref, own_ref, sems = refs
    step = 1024
    chunks = down_ref.shape[0] // step
    copies = []
    for i in range(chunks):
        at = pl.ds(i * step, step)
        copies.append(pltpu.make_async_copy(down_hbm.at[at], down_ref.at[at], sems.at[i]))
    copies.append(pltpu.make_async_copy(gt_hbm.at[: gt_ref.shape[0]], gt_ref, sems.at[chunks]))
    copies.append(pltpu.make_async_copy(own_hbm, own_ref, sems.at[chunks + 1]))
    for copy in copies:
        copy.start()
    low = low_ref[...]
    for i in range(chunks):
        copies[i].wait()
        at = slice(i * step, (i + 1) * step)
        acc_ref[at, :] = lax.dot_general(
            down_ref[at, :], low, LANES_OVER, preferred_element_type=F32
        )
    copies[chunks].wait()
    copies[chunks + 1].wait()

    def pair(i, carry):
        slots = [4 * i + n for n in range(4)]
        spread(table, gt_ref, acc_ref, [(own_ref[s], 0, 0, s, s + PAIRS) for s in slots])
        return carry

    lax.fori_loop(0, PAIRS // 4, pair, 0)
    token_ref[...] = jnp.zeros_like(token_ref)


def input_kernel(place, table, acc_in, *refs):
    from_hbm = refs[:5]
    out_hbm, acc_ref, token_ref, gt_ref, values, out_ref, sems = refs[5:]
    most = from_hbm[0].shape[0]
    width = from_hbm[1].shape[0]
    to_vmem = [gt_ref.at[width:most], gt_ref.at[most:]] + [values.at[n] for n in range(T - 1)]
    here = [from_hbm[0].at[width:], *from_hbm[1:]]
    copies = [
        pltpu.make_async_copy(there, at, sems.at[n])
        for n, (there, at) in enumerate(zip(here, to_vmem))
    ]
    for copy in copies:
        copy.start()
    for copy in copies:
        copy.wait()

    def pair(i, carry):
        parts = []
        for s0 in (2 * i, 2 * i + 1):
            for m in range(1, T):
                k = place[m]
                parts.append((values[m - 1, s0], k, k * (width // BLK), s0, s0 + PAIRS))
        spread(table, gt_ref, acc_ref, parts)
        return carry

    lax.fori_loop(0, PAIRS // 2, pair, 0)
    gives = []
    step = 1024
    for j in range(0, out_ref.shape[1], step):
        for i in range(j, j + step, 128):
            out_ref[:, i : i + 128] = acc_ref[i : i + 128, :].T.astype(BF16)
        at = pl.ds(j, step)
        gives.append(
            pltpu.make_async_copy(out_ref.at[:, at], out_hbm.at[:, at], sems.at[5 + j // step])
        )
        gives[-1].start()
    for give in gives:
        give.wait()
    token_ref[...] = jnp.zeros_like(token_ref)


def ring(shift_of_core):
    def place(z, c):
        return (z // T * C + c) * T + z % T

    n = ZH * T
    return [
        (place(z, c), place((z + shift_of_core[c]) % n, c)) for z in range(n) for c in range(C)
    ]


def swap(array, axis="c"):
    return lax.ppermute(array, axis, [(0, 1), (1, 0)])


def cross(array, k):
    return lax.ppermute(array, "t", [(i, i ^ k) for i in range(T)])


def call(kernel, name, outs, in_specs, *args, out_specs=None, scratch=(), room=16, **grid):
    return pl.pallas_call(
        kernel,
        out_shape=outs,
        in_specs=in_specs,
        out_specs=out_specs if out_specs is not None else jax.tree.map(lambda _: whole(), outs),
        scratch_shapes=scratch,
        compiler_params=pltpu.CompilerParams(vmem_limit_bytes=room * MIB),
        cost_estimate=pl.CostEstimate(
            flops=int(GUESS.get(name, 0) * 1000000000) + 1024, bytes_accessed=1024, transcendentals=0
        ),
        name=name,
        **grid,
    )(*args)


def per_device(x_own, acts, grad, down, up, values, slot_rows, slot_cols, count):
    zh, c, t = lax.axis_index("zh"), lax.axis_index("c"), lax.axis_index("t")
    feat, width, rank = x_own.shape[1], grad.shape[1], up.shape[0]
    place = jnp.stack(
        [c, t ^ ((t - 1) % T), t ^ ((t + 1) % T), 2 + 0 * t, t, zh]
    ).astype(jnp.int32)
    rows = TOK + 16
    shape = jax.ShapeDtypeStruct

    given = call(
        front_kernel, "front",
        (shape((rows, rank), BF16),) * T + (shape((TOK, width), BF16),) * T,
        [scalars()] * 2 + [anywhere()] * 4, place, count, grad, up, slot_rows, slot_cols,
        out_specs=(anywhere(),) * (2 * T), room=56,
        scratch=[
            pltpu.VMEM(grad.shape, BF16),
            pltpu.VMEM(up.shape, BF16),
            pltpu.VMEM((1, SLOTS), jnp.int32),
            pltpu.VMEM((1, SLOTS), jnp.int32),
            pltpu.VMEM((T * TOK, rank), BF16),
            pltpu.VMEM((T, rows, rank), BF16),
            pltpu.SemaphoreType.DMA((4 + 2 * T,)),
        ],
    )
    parts, near = given[:T], given[T:]
    parts = [parts[0]] + [cross(parts[k], k) for k in (1, 2, 3)]
    near = [near[0]] + [cross(near[k], k) for k in (1, 2, 3)]

    xt = call(
        turn_kernel, "turn_input", shape((feat, TOK), BF16),
        [anywhere()] * 2, x_own, given[T],
        scratch=[pltpu.VMEM(x_own.shape, BF16), pltpu.SemaphoreType.DMA((8,))],
    )
    xt_far = swap(xt)

    half = shape((rank // C, width), BF16)
    up_keep, up_give = call(
        up_kernel, "up_part", (shape(half.shape, F32), half), [scalars()] + [anywhere()] * 2,
        place, grad, acts,
        scratch=[
            pltpu.VMEM(grad.shape, BF16),
            pltpu.VMEM(acts.shape, BF16),
            pltpu.SemaphoreType.DMA((2,)),
        ],
    )
    up_got = swap(up_give)

    low, table = call(
        low_kernel, "low", (shape((TOK, rank), BF16), shape((8 * T, rank), jnp.int32)),
        [whole()] * T + [anywhere()], *parts, up_give,
    )
    low_far = swap(low)

    size = XY, ZH * 128 + ZH * 4 * width // rank, rank
    down_part = call(
        down_kernel, "down_part", shape(size, BF16), [scalars()] + [whole()] * 6,
        place, xt, xt_far, low, low_far, up_keep, up_got,
    )
    down_all = lax.all_to_all(down_part, ("y", "x"), 0, 0, tiled=True)
    def delta_call(pieces, *before):
        n = len(pieces)
        return call(
            functools.partial(delta_kernel, pieces), "delta_last" if before else "delta_most",
            (shape((XY, T, BLK, 2 * BLK), BF16), shape((n * width, TOK), BF16)),
            [scalars()] * 2 + [whole()] * (2 + 2 * n) + [anywhere()] * len(before),
            place, table, xt, xt_far, *[near[k] for k in pieces], *[far[k] for k in pieces],
            *before,
            out_specs=(anywhere(), anywhere()), room=24,
            scratch=[
                pltpu.VMEM((XY, n, BLK, 2 * BLK), BF16),
                pltpu.VMEM((n * width, TOK), BF16),
                pltpu.VMEM((width, 256 * n), BF16),
                pltpu.SemaphoreType.DMA((2,)),
            ],
            input_output_aliases={4 + 2 * n: 0} if before else {},
        )

    far = [swap(near[k]) for k in (0, 1, 2)]
    delta_most, grad_most = delta_call((0, 1, 2))
    token = shape((8, 128), F32)
    packed = call(
        pack_kernel, "pack", shape((PAIRS, BLK, 2 * BLK), BF16), [whole()], values[0],
    )
    acc, token = call(
        dense_kernel, "dense", (shape((feat, TOK), F32), token),
        [scalars(), whole()] + [anywhere()] * 3, table, low, down, grad_most, packed, room=24,
        scratch=[
            pltpu.VMEM(down.shape, BF16),
            pltpu.VMEM((width, TOK), BF16),
            pltpu.VMEM((PAIRS, BLK, 2 * BLK), BF16),
            pltpu.SemaphoreType.DMA((10,)),
        ],
    )

    near[3] = call(
        pass_kernel, "gate", shape((TOK, width), BF16), [anywhere(), whole()], near[3], token,
        out_specs=anywhere(), input_output_aliases={0: 0},
    )
    far.append(swap(near[3]))
    delta_full, grad_last = delta_call((3,), delta_most)
    delta_part = call(
        pass_kernel, "join", shape((XY, T, BLK, 2 * BLK), BF16), [anywhere()] * 2,
        delta_full, down_all,
        out_specs=anywhere(), input_output_aliases={0: 0},
    )
    delta_all = lax.all_to_all(delta_part, ("y", "x"), 0, 0, tiled=True)

    down_keep, down_give, up_sum = call(
        down_sum_kernel, "down_sum",
        (
            shape((128, rank), F32),
            shape((128 + 4 * width // rank, rank), BF16),
            shape((4, width), F32),
        ),
        [scalars(), whole()], place, down_all,
    )
    down_half, up_grad = call(
        down_half_kernel, "down_half", (shape((128, rank), BF16), shape((4, width), F32)),
        [whole()] * 3, down_keep, swap(down_give, "zh"), up_sum,
    )
    down_grad = call(
        down_last_kernel, "down_last", shape((128, rank), F32), [whole()] * T,
        down_half, *[cross(down_half, k) for k in (1, 2, 3)],
    )


    axes = ("zh", "t")
    got = [
        lax.ppermute(packed, axes, [(i, (i + 1) % (ZH * T)) for i in range(ZH * T)]),
        lax.ppermute(packed, axes, [(i, (i - 1) % (ZH * T)) for i in range(ZH * T)]),
        lax.ppermute(packed, ("zh", "c", "t"), ring((2, -2))),
    ]
    got = call(
        pass_kernel, "values", (shape(packed.shape, BF16),) * 3, [anywhere()] * 3, *got,
        out_specs=(anywhere(),) * 3, input_output_aliases={0: 0, 1: 1, 2: 2},
    )
    grad_input, _, token = call(
        input_kernel, "grad_input",
        (shape((TOK, feat), BF16), shape((feat, TOK), F32), shape((8, 128), F32)),
        [scalars()] * 2 + [whole()] + [anywhere()] * 5,
        place, table, acc, grad_most, grad_last, *got, room=24,
        out_specs=(anywhere(), whole(), whole()),
        scratch=[
            pltpu.VMEM((T * width, TOK), BF16),
            pltpu.VMEM((T - 1, PAIRS, BLK, 2 * BLK), BF16),
            pltpu.VMEM((TOK, feat), BF16),
            pltpu.SemaphoreType.DMA((5 + feat // 1024,)),
        ],
        input_output_aliases={2: 1},
    )

    stage = call(
        stage_kernel, "stage", shape((ZH * T, BLK, 128), BF16),
        [scalars()] + [whole()] * 2 + [anywhere()], place, delta_all, down_half, got[0],
        scratch=[pltpu.VMEM((T, BLK, 2 * BLK), F32)],
    )

    stage_all = lax.all_to_all(stage, ("zh", "t"), 0, 0, tiled=True)
    delta_one = call(
        last_kernel, "last", shape((PAIRS, BLK, 2 * BLK), BF16), [whole()] * 2, stage_all, token,
    )
    delta_full = lax.all_to_all(delta_one, ("y", "x", "c"), 0, 0, tiled=True)
    grad_delta = call(
        unpack_kernel, "unpack", shape((SLOTS, BLK, BLK), F32), [whole()], delta_full
    )[None]
    return down_grad, up_grad, grad_delta, grad_input


def solution(mesh):
    fine = Mesh(mesh.devices.reshape(ZH, Y, X, C, T), ALL)
    return jax.shard_map(
        per_device,
        mesh=fine,
        in_specs=(
            P(ALL, None),
            P(DP, None),
            P(DP, "t"),
            P(),
            P(None, "t"),
            P("t", None, None, None),
            P("t", None),
            P("t", None),
            P("t"),
        ),
        out_specs=(
            P(DP, None),
            P(DP, "t"),
            P("t", None, None, None),
            P(ALL, None),
        ),
        check_vma=False,
    )
```

```python
import functools

import jax
import jax.numpy as jnp
from jax import lax
from jax.experimental import pallas as pl
from jax.experimental.pallas import tpu as pltpu
from jax.sharding import Mesh, PartitionSpec as P

F32 = jnp.float32
BF16 = jnp.bfloat16
ZH, Y, X, C, T = 2, 4, 4, 2, 4
XY = Y * X
DP = ("zh", "y", "x", "c")
ALL = DP + ("t",)
BLK = 64
TOK = 128
SLOTS = 64
PAIRS = SLOTS // 2
LANES_OVER = (((1,), (1,)), ((), ()))
MIB = 1024 * 1024


GUESS = {"delta_last": 0.0, "delta_most": 0.0, "low": 10.0, "grad_input": 0.0, "stage": 0.0, "pack": 0.0, "values": 10.0, "gate": 12.0}


def whole():
    return pl.BlockSpec(memory_space=pltpu.VMEM)


def scalars():
    return pl.BlockSpec(memory_space=pltpu.SMEM)


def anywhere():
    return pl.BlockSpec(memory_space=pl.ANY)


def aligned(index, size):
    return pl.ds(pl.multiple_of(index * size, size), size)


def turn_kernel(x_hbm, after_ref, out_ref, x_ref, sems):
    step = x_ref.shape[1] // 8
    copies = []
    for i in range(8):
        at = pl.ds(i * step, step)
        copies.append(pltpu.make_async_copy(x_hbm.at[:, at], x_ref.at[:, at], sems.at[i]))
    for copy in copies:
        copy.start()
    for i in range(8):
        copies[i].wait()
        for j in range(i * step, i * step + step, 128):
            out_ref[j : j + 128, :] = x_ref[:, j : j + 128].T


def front_kernel(place, count, *refs):
    from_hbm, lows, pieces = refs[:4], refs[4 : 4 + T], refs[4 + T : 4 + 2 * T]
    grad_ref, up_ref, rows_ref, cols_ref, low_ref, ext_ref, sems = refs[4 + 2 * T :]
    copies = [
        pltpu.make_async_copy(there, here, sems.at[i])
        for i, (there, here) in enumerate(zip(from_hbm, (grad_ref, up_ref, rows_ref, cols_ref)))
    ]
    for copy in copies:
        copy.start()
    copies[0].wait()
    gives = []
    for k in range(T):
        at = pl.ds(pl.multiple_of((place[4] ^ k) * TOK, TOK), TOK)
        gives.append(pltpu.make_async_copy(grad_ref.at[at], pieces[k], sems.at[4 + k]))
    for give in gives:
        give.start()
    for copy in copies[1:]:
        copy.wait()
    low_ref[...] = lax.dot_general(
        grad_ref[...], up_ref[...], LANES_OVER, preferred_element_type=F32
    ).astype(BF16)
    line = jnp.concatenate(
        [rows_ref[...], cols_ref[...], jnp.full((1, 2 * SLOTS), count[0], jnp.int32)], axis=1
    ).astype(F32)
    line = jnp.broadcast_to(line, (16, line.shape[1])).astype(BF16)
    for k in range(T):
        ext_ref[k, :TOK] = low_ref[aligned(place[4] ^ k, TOK), :]
        ext_ref[k, TOK:] = line
        gives.append(pltpu.make_async_copy(ext_ref.at[k], lows[k], sems.at[4 + T + k]))
        gives[-1].start()
    for give in gives:
        give.wait()


def up_kernel(place, grad_hbm, acts_hbm, keep_ref, give_ref, grad_ref, acts_ref, sems):
    copies = [
        pltpu.make_async_copy(acts_hbm, acts_ref, sems.at[0]),
        pltpu.make_async_copy(grad_hbm, grad_ref, sems.at[1]),
    ]
    for copy in copies:
        copy.start()
    copies[0].wait()
    rank = acts_ref.shape[1]
    half = rank // C
    here = lax.broadcasted_iota(jnp.int32, (rank, rank), 1)
    core, yx, zh = (here >> 7) ^ place[0], (here >> 3) & (XY - 1), (here >> 2) & 1
    order = lax.broadcasted_iota(jnp.int32, (rank, rank), 0) == (
        (((zh * XY + yx) * C + core) << 2) + (here & 3)
    )
    order = jnp.where(order, 1.0, 0.0).astype(BF16)
    acts = jnp.dot(acts_ref[...], order, preferred_element_type=F32).astype(BF16)
    copies[1].wait()
    step = 512

    def columns(i, carry):
        part = lax.dot_general(
            acts, grad_ref[:, aligned(i, step)], (((0,), (0,)), ((), ())),
            preferred_element_type=F32,
        )
        keep_ref[:, aligned(i, step)] = part[:half]
        give_ref[:, aligned(i, step)] = part[half:].astype(BF16)
        return carry

    lax.fori_loop(0, grad_ref.shape[1] // step, columns, 0, unroll=2)


def low_kernel(*refs):
    low_ref, table_ref = refs[-2:]
    total = refs[0][:TOK].astype(F32)
    for piece in refs[1:T]:
        total += piece[:TOK].astype(F32)
    low_ref[...] = total.astype(BF16)
    for k in range(T):
        table_ref[k * 8 : k * 8 + 8] = refs[k][TOK:].astype(F32).astype(jnp.int32)[:8]


def pass_kernel(*refs):
    pass


def pack_kernel(values_ref, out_ref):
    def one(p, carry):
        out_ref[p] = jnp.concatenate([values_ref[p], values_ref[p + PAIRS]], axis=1)
        return carry

    lax.fori_loop(0, PAIRS, one, 0, unroll=4)


def down_sum_kernel(place, down_ref, keep_ref, give_ref, up_ref):
    def total(at):
        part = down_ref[0, at, :].astype(F32)
        for i in range(1, XY):
            part += down_ref[i, at, :].astype(F32)
        return part

    zh = place[5]
    keep_ref[...] = total(aligned(zh, 128))
    give_ref[:128] = total(aligned(1 - zh, 128)).astype(BF16)
    up = total(slice(256, None))
    rank = up.shape[1]
    give = []
    for j in range(up.shape[0] // 8):
        low, high = up[j * 8 : j * 8 + 4], up[j * 8 + 4 : j * 8 + 8]
        up_ref[:, j * rank : (j + 1) * rank] = jnp.where(zh == 0, low, high)
        give.append(jnp.where(zh == 0, high, low))
    give_ref[128:] = jnp.concatenate(give, axis=0).astype(BF16)


def down_half_kernel(keep_ref, far_ref, up_ref, out_ref, up_out_ref):
    out_ref[...] = (keep_ref[...] + far_ref[:128].astype(F32)).astype(BF16)
    up = far_ref[128:].astype(F32)
    rank = up.shape[1]
    for j in range(up.shape[0] // 4):
        at = slice(j * rank, (j + 1) * rank)
        up_out_ref[:, at] = up_ref[:, at] + up[j * 4 : j * 4 + 4]


def down_last_kernel(*refs):
    total = refs[0][...].astype(F32)
    for part in refs[1:T]:
        total += part[...].astype(F32)
    refs[-1][...] = total


def stage_kernel(place, delta_ref, *refs):
    out_ref, sum_ref = refs[-2:]
    for k in range(T):
        total = delta_ref[0, k].astype(F32)
        for i in range(1, XY):
            total += delta_ref[i, k].astype(F32)
        sum_ref[k] = total
    for t in range(T):
        part = sum_ref[place[4] ^ t].astype(BF16)
        for zh in range(ZH):
            out_ref[zh * T + t] = part


def last_kernel(parts_ref, after_ref, delta_ref):
    total = parts_ref[0].astype(F32)
    for i in range(1, ZH * T):
        total += parts_ref[i].astype(F32)
    delta = total.astype(BF16)
    for p in range(PAIRS):
        delta_ref[p] = delta


def unpack_kernel(pairs_ref, out_ref):
    def one(p, carry):
        pair = pairs_ref[p].astype(F32)
        out_ref[p] = pair[:, :BLK]
        out_ref[p + PAIRS] = pair[:, BLK:]
        return carry

    lax.fori_loop(0, PAIRS, one, 0, unroll=4)


def down_kernel(place, xt_ref, xt_far_ref, low_ref, low_far_ref, up_ref, up_far_ref, out_ref):
    low, low_far = low_ref[...], low_far_ref[...]
    core = place[0]
    rank = low.shape[1]

    def block(i, carry):
        for zh in range(ZH):
            at = aligned((zh * XY + i) * C + core, 128)
            total = jnp.dot(xt_ref[at, :], low, preferred_element_type=F32)
            total += jnp.dot(xt_far_ref[at, :], low_far, preferred_element_type=F32)
            out_ref[i, zh * 128 : (zh + 1) * 128] = total.astype(BF16)
        return carry

    lax.fori_loop(0, XY, block, 0, unroll=4)
    for i in range(0, XY, 2):
        at = slice(i * 8, i * 8 + 16)
        for j in range(0, up_ref.shape[1] // rank, 2):
            two = []
            for n in (j, j + 1):
                lanes = slice(n * rank, (n + 1) * rank)
                two.append(up_ref[at, lanes] + up_far_ref[at, lanes].astype(F32))
            for n in range(2):
                both = [part[n * 8 : n * 8 + 8] for part in two]
                out_ref[i + n, 256 + j * 8 : 256 + j * 8 + 16] = jnp.concatenate(both, 0).astype(BF16)


def delta_kernel(pieces, place, table, xt_ref, xt_far_ref, *refs):
    n = len(pieces)
    near, far = refs[:n], refs[n : 2 * n]
    all_ref, grad_ref, out_ref, gt_ref, both_ref, sems = refs[-6:]
    width = near[0].shape[1]
    core = place[0]
    for j in range(n):

        def turn(i, carry, j=j):
            at = pl.ds(pl.multiple_of(i * 128, 128), 128)
            own = near[j][:, at].T
            both_ref[at, j * 256 : j * 256 + 128] = own
            both_ref[at, j * 256 + 128 : j * 256 + 256] = far[j][:, at].T
            gt_ref[pl.ds(pl.multiple_of(j * width + i * 128, 128), 128), :] = own
            return carry

        lax.fori_loop(0, width // 128, turn, 0, unroll=4)
    keep = pltpu.make_async_copy(gt_ref, grad_ref, sems.at[0])
    keep.start()

    lane = lax.broadcasted_iota(jnp.int32, (BLK, 2 * BLK), 1)

    def rows_of(index):
        return jnp.concatenate(
            [xt_ref[aligned(index, BLK), :], xt_far_ref[aligned(index, BLK), :]], axis=1
        )

    def pair(i, carry):
        s0 = i * C + core
        s1 = s0 + PAIRS
        for j, k in enumerate(pieces):
            xt = jnp.concatenate([rows_of(table[8 * k, s0]), rows_of(table[8 * k, s1])], axis=0)
            gt = jnp.concatenate(
                [
                    both_ref[aligned(table[8 * k, SLOTS + s], BLK), j * 256 : j * 256 + 256]
                    for s in (s0, s1)
                ],
                axis=0,
            )
            full = lax.dot_general(xt, gt, LANES_OVER, preferred_element_type=F32)
            live = jnp.where(lane < BLK, s0, s1) < table[8 * k, 2 * SLOTS]
            both = jnp.where(lane < BLK, full[:BLK], full[BLK:])
            out_ref[i, j] = jnp.where(live, both, 0.0).astype(BF16)
        return carry

    lax.fori_loop(0, XY, pair, 0, unroll=4)
    give = pltpu.make_async_copy(out_ref, all_ref.at[:, pieces[0] : pieces[0] + n], sems.at[1])
    give.start()
    keep.wait()
    give.wait()


def spread(table, gt_ref, acc_ref, parts):
    lane = lax.broadcasted_iota(jnp.int32, (BLK, 2 * BLK), 1)
    done = []
    for v, k, base, s0, s1 in parts:
        zero = jnp.zeros_like(v)
        live = table[8 * k, 2 * SLOTS]
        top = jnp.where((lane < BLK) & (s0 < live), v, zero)
        bottom = jnp.where((lane >= BLK) & (s1 < live), v, zero)
        gt = jnp.concatenate(
            [gt_ref[aligned(table[8 * k, SLOTS + s] + base, BLK), :] for s in (s0, s1)], axis=0
        )
        both = jnp.concatenate([top, bottom], axis=0)
        done.append(jnp.dot(both, gt, preferred_element_type=F32))
    for (_, k, _, s0, s1), part in zip(parts, done):
        for s, add in ((s0, part[:BLK]), (s1, part[BLK:])):
            at = aligned(table[8 * k, s], BLK)
            acc_ref[at, :] = acc_ref[at, :] + add


def dense_kernel(table, low_ref, down_hbm, gt_hbm, own_hbm, acc_ref, token_ref, *refs):
    down_ref, gt_ref, own_ref, sems = refs
    step = 1024
    chunks = down_ref.shape[0] // step
    copies = []
    for i in range(chunks):
        at = pl.ds(i * step, step)
        copies.append(pltpu.make_async_copy(down_hbm.at[at], down_ref.at[at], sems.at[i]))
    copies.append(pltpu.make_async_copy(gt_hbm.at[: gt_ref.shape[0]], gt_ref, sems.at[chunks]))
    copies.append(pltpu.make_async_copy(own_hbm, own_ref, sems.at[chunks + 1]))
    for copy in copies:
        copy.start()
    low = low_ref[...]
    for i in range(chunks):
        copies[i].wait()
        at = slice(i * step, (i + 1) * step)
        acc_ref[at, :] = lax.dot_general(
            down_ref[at, :], low, LANES_OVER, preferred_element_type=F32
        )
    copies[chunks].wait()
    copies[chunks + 1].wait()

    def pair(i, carry):
        slots = [4 * i + n for n in range(4)]
        spread(table, gt_ref, acc_ref, [(own_ref[s], 0, 0, s, s + PAIRS) for s in slots])
        return carry

    lax.fori_loop(0, PAIRS // 4, pair, 0)
    token_ref[...] = jnp.zeros_like(token_ref)


def input_kernel(place, table, acc_hbm, *refs):
    from_hbm = refs[:5]
    out_hbm, token_ref, acc_ref, gt_ref, values, out_ref, sems = refs[5:]
    most = from_hbm[0].shape[0]
    width = from_hbm[1].shape[0]
    to_vmem = [gt_ref.at[width:most], gt_ref.at[most:]] + [values.at[n] for n in range(T - 1)]
    here = [from_hbm[0].at[width:], *from_hbm[1:], acc_hbm]
    to_vmem.append(acc_ref)
    copies = [
        pltpu.make_async_copy(there, at, sems.at[n])
        for n, (there, at) in enumerate(zip(here, to_vmem))
    ]
    for copy in copies:
        copy.start()
    for copy in copies:
        copy.wait()

    def pair(i, carry):
        parts = []
        for s0 in (2 * i, 2 * i + 1):
            for m in range(1, T):
                k = place[m]
                parts.append((values[m - 1, s0], k, k * (width // BLK), s0, s0 + PAIRS))
        spread(table, gt_ref, acc_ref, parts)
        return carry

    lax.fori_loop(0, PAIRS // 2, pair, 0)
    gives = []
    step = 1024
    for j in range(0, out_ref.shape[1], step):
        for i in range(j, j + step, 128):
            out_ref[:, i : i + 128] = acc_ref[i : i + 128, :].T.astype(BF16)
        at = pl.ds(j, step)
        gives.append(
            pltpu.make_async_copy(out_ref.at[:, at], out_hbm.at[:, at], sems.at[6 + j // step])
        )
        gives[-1].start()
    for give in gives:
        give.wait()
    token_ref[...] = jnp.zeros_like(token_ref)


def ring(shift_of_core):
    def place(z, c):
        return (z // T * C + c) * T + z % T

    n = ZH * T
    return [
        (place(z, c), place((z + shift_of_core[c]) % n, c)) for z in range(n) for c in range(C)
    ]


def swap(array, axis="c"):
    return lax.ppermute(array, axis, [(0, 1), (1, 0)])


def cross(array, k):
    return lax.ppermute(array, "t", [(i, i ^ k) for i in range(T)])


def call(kernel, name, outs, in_specs, *args, out_specs=None, scratch=(), room=16, **grid):
    return pl.pallas_call(
        kernel,
        out_shape=outs,
        in_specs=in_specs,
        out_specs=out_specs if out_specs is not None else jax.tree.map(lambda _: whole(), outs),
        scratch_shapes=scratch,
        compiler_params=pltpu.CompilerParams(vmem_limit_bytes=room * MIB),
        cost_estimate=pl.CostEstimate(
            flops=int(GUESS.get(name, 0) * 1000000000) + 1024, bytes_accessed=1024, transcendentals=0
        ),
        name=name,
        **grid,
    )(*args)


def per_device(x_own, acts, grad, down, up, values, slot_rows, slot_cols, count):
    zh, c, t = lax.axis_index("zh"), lax.axis_index("c"), lax.axis_index("t")
    feat, width, rank = x_own.shape[1], grad.shape[1], up.shape[0]
    place = jnp.stack(
        [c, t ^ ((t - 1) % T), t ^ ((t + 1) % T), 2 + 0 * t, t, zh]
    ).astype(jnp.int32)
    rows = TOK + 16
    shape = jax.ShapeDtypeStruct

    given = call(
        front_kernel, "front",
        (shape((rows, rank), BF16),) * T + (shape((TOK, width), BF16),) * T,
        [scalars()] * 2 + [anywhere()] * 4, place, count, grad, up, slot_rows, slot_cols,
        out_specs=(anywhere(),) * (2 * T), room=56,
        scratch=[
            pltpu.VMEM(grad.shape, BF16),
            pltpu.VMEM(up.shape, BF16),
            pltpu.VMEM((1, SLOTS), jnp.int32),
            pltpu.VMEM((1, SLOTS), jnp.int32),
            pltpu.VMEM((T * TOK, rank), BF16),
            pltpu.VMEM((T, rows, rank), BF16),
            pltpu.SemaphoreType.DMA((4 + 2 * T,)),
        ],
    )
    parts, near = given[:T], given[T:]
    parts = [parts[0]] + [cross(parts[k], k) for k in (1, 2, 3)]
    near = [near[0]] + [cross(near[k], k) for k in (1, 2, 3)]

    xt = call(
        turn_kernel, "turn_input", shape((feat, TOK), BF16),
        [anywhere()] * 2, x_own, given[T],
        scratch=[pltpu.VMEM(x_own.shape, BF16), pltpu.SemaphoreType.DMA((8,))],
    )
    xt_far = swap(xt)

    half = shape((rank // C, width), BF16)
    up_keep, up_give = call(
        up_kernel, "up_part", (shape(half.shape, F32), half), [scalars()] + [anywhere()] * 2,
        place, grad, acts,
        scratch=[
            pltpu.VMEM(grad.shape, BF16),
            pltpu.VMEM(acts.shape, BF16),
            pltpu.SemaphoreType.DMA((2,)),
        ],
    )
    up_got = swap(up_give)

    low, table = call(
        low_kernel, "low", (shape((TOK, rank), BF16), shape((8 * T, rank), jnp.int32)),
        [whole()] * T + [anywhere()], *parts, up_give,
    )
    low_far = swap(low)

    size = XY, ZH * 128 + ZH * 4 * width // rank, rank
    down_part = call(
        down_kernel, "down_part", shape(size, BF16), [scalars()] + [whole()] * 6,
        place, xt, xt_far, low, low_far, up_keep, up_got,
    )
    down_all = lax.all_to_all(down_part, ("y", "x"), 0, 0, tiled=True)
    def delta_call(pieces, *before):
        n = len(pieces)
        return call(
            functools.partial(delta_kernel, pieces), "delta_last" if before else "delta_most",
            (shape((XY, T, BLK, 2 * BLK), BF16), shape((n * width, TOK), BF16)),
            [scalars()] * 2 + [whole()] * (2 + 2 * n) + [anywhere()] * len(before),
            place, table, xt, xt_far, *[near[k] for k in pieces], *[far[k] for k in pieces],
            *before,
            out_specs=(anywhere(), anywhere()), room=24,
            scratch=[
                pltpu.VMEM((XY, n, BLK, 2 * BLK), BF16),
                pltpu.VMEM((n * width, TOK), BF16),
                pltpu.VMEM((width, 256 * n), BF16),
                pltpu.SemaphoreType.DMA((2,)),
            ],
            input_output_aliases={4 + 2 * n: 0} if before else {},
        )

    far = [swap(near[k]) for k in (0, 1, 2)]
    delta_most, grad_most = delta_call((0, 1, 2))
    token = shape((8, 128), F32)
    packed = call(
        pack_kernel, "pack", shape((PAIRS, BLK, 2 * BLK), BF16), [whole()], values[0],
    )
    acc, token = call(
        dense_kernel, "dense", (shape((feat, TOK), F32), token),
        [scalars(), whole()] + [anywhere()] * 3, table, low, down, grad_most, packed, room=24,
        scratch=[
            pltpu.VMEM(down.shape, BF16),
            pltpu.VMEM((width, TOK), BF16),
            pltpu.VMEM((PAIRS, BLK, 2 * BLK), BF16),
            pltpu.SemaphoreType.DMA((10,)),
        ],
    )

    near[3] = call(
        pass_kernel, "gate", shape((TOK, width), BF16), [anywhere(), whole()], near[3], token,
        out_specs=anywhere(), input_output_aliases={0: 0},
    )
    far.append(swap(near[3]))
    delta_full, grad_last = delta_call((3,), delta_most)
    delta_part = call(
        pass_kernel, "join", shape((XY, T, BLK, 2 * BLK), BF16), [anywhere()] * 2,
        delta_full, down_all,
        out_specs=anywhere(), input_output_aliases={0: 0},
    )
    delta_all = lax.all_to_all(delta_part, ("y", "x"), 0, 0, tiled=True)

    down_keep, down_give, up_sum = call(
        down_sum_kernel, "down_sum",
        (
            shape((128, rank), F32),
            shape((128 + 4 * width // rank, rank), BF16),
            shape((4, width), F32),
        ),
        [scalars(), whole()], place, down_all,
    )
    down_half, up_grad = call(
        down_half_kernel, "down_half", (shape((128, rank), BF16), shape((4, width), F32)),
        [whole()] * 3, down_keep, swap(down_give, "zh"), up_sum,
    )
    down_grad = call(
        down_last_kernel, "down_last", shape((128, rank), F32), [whole()] * T,
        down_half, *[cross(down_half, k) for k in (1, 2, 3)],
    )


    axes = ("zh", "t")
    got = [
        lax.ppermute(packed, axes, [(i, (i + 1) % (ZH * T)) for i in range(ZH * T)]),
        lax.ppermute(packed, axes, [(i, (i - 1) % (ZH * T)) for i in range(ZH * T)]),
        lax.ppermute(packed, ("zh", "c", "t"), ring((2, -2))),
    ]
    got = call(
        pass_kernel, "values", (shape(packed.shape, BF16),) * 3, [anywhere()] * 3, *got,
        out_specs=(anywhere(),) * 3, input_output_aliases={0: 0, 1: 1, 2: 2},
    )
    grad_input, token = call(
        input_kernel, "grad_input",
        (shape((TOK, feat), BF16), shape((8, 128), F32)),
        [scalars()] * 2 + [anywhere()] * 6,
        place, table, acc, grad_most, grad_last, *got, room=24,
        out_specs=(anywhere(), whole()),
        scratch=[
            pltpu.VMEM((feat, TOK), F32),
            pltpu.VMEM((T * width, TOK), BF16),
            pltpu.VMEM((T - 1, PAIRS, BLK, 2 * BLK), BF16),
            pltpu.VMEM((TOK, feat), BF16),
            pltpu.SemaphoreType.DMA((6 + feat // 1024,)),
        ],
    )

    stage = call(
        stage_kernel, "stage", shape((ZH * T, BLK, 128), BF16),
        [scalars()] + [whole()] * 2 + [anywhere()], place, delta_all, down_half, got[0],
        scratch=[pltpu.VMEM((T, BLK, 2 * BLK), F32)],
    )

    stage_all = lax.all_to_all(stage, ("zh", "t"), 0, 0, tiled=True)
    delta_one = call(
        last_kernel, "last", shape((PAIRS, BLK, 2 * BLK), BF16), [whole()] * 2, stage_all, token,
    )
    delta_full = lax.all_to_all(delta_one, ("y", "x", "c"), 0, 0, tiled=True)
    grad_delta = call(
        unpack_kernel, "unpack", shape((SLOTS, BLK, BLK), F32), [whole()], delta_full
    )[None]
    return down_grad, up_grad, grad_delta, grad_input


def solution(mesh):
    fine = Mesh(mesh.devices.reshape(ZH, Y, X, C, T), ALL)
    return jax.shard_map(
        per_device,
        mesh=fine,
        in_specs=(
            P(ALL, None),
            P(DP, None),
            P(DP, "t"),
            P(),
            P(None, "t"),
            P("t", None, None, None),
            P("t", None),
            P("t", None),
            P("t"),
        ),
        out_specs=(
            P(DP, None),
            P(DP, "t"),
            P("t", None, None, None),
            P(ALL, None),
        ),
        check_vma=False,
    )
```
